512 devices in a mesh: gx: 16 (over x, y_lo, core), gy: 32 (over z, y_hi).
Axes of the slice: x: 4, y: 8 (y_hi: 4, y_lo: 2; y = y_hi * 2 + y_lo), z: 8, core: 2. Of those that a mesh axis runs over, the one named last changes fastest.
Arguments:
- features: bfloat16 [16, 32, 16, 64, 192], P('gx', 'gy'), may hold values from -45 to 45
- cotangent: bfloat16 [16, 32, 16, 64, 192], P('gx', 'gy'), may hold values from -6 to 6
- counts: int32 [16, 32], P('gx', 'gy'), may hold values from 2 to 16, as said below
- neighbours: int32 [16, 32, 16, 27], P('gx', 'gy'), may hold values from 0 to 56, as said below
- send_x: int32 [16, 32, 2, 8], P('gx', 'gy'), may hold values from 0 to 16, as said below
- send_y: int32 [16, 32, 2, 12], P('gx', 'gy'), may hold values from 0 to 32, as said below
- action: float32 [128], replicated, may hold values from -6 to 6
- conv_weight: bfloat16 [192, 27, 192], replicated, may hold values from -0.078125 to 0.078125
- film_weight: float32 [128, 384], replicated, may hold values from -0.5 to 0.5
Outputs:
- output: bfloat16 [16, 32, 16, 64, 192], P('gx', 'gy')
- grad_features: bfloat16 [16, 32, 16, 64, 192], P('gx', 'gy')
- grad_conv_weight: float32 [192, 27, 192], P('gx')
- grad_film_weight: float32 [128, 384], replicated
The draws below stay inside these ranges and needn't reach their ends.
Inputs may be any that keep to these rules, and one draw needn't show every extreme that they name: Slots below counts[i, j] hold the tile's active blocks, the others are unused; some tile has 16. `neighbours`: rows index E of the tile: local slots, the zero block at 16, 8 rows from the lower and 8 from the upper x neighbour, 12 from the lower and 12 from the upper y neighbour. 16 where the neighbouring block is inactive or outside the scene, and in every row of unused slots. `send_x`: [.., 0, :] the active blocks of the tile's lowest x layer of blocks, [.., 1, :] of its highest, as slot numbers, packed to the front, filled with 16; where 16 >= 8, some tile's list has no filler. `send_y`: [.., 0, :] the active blocks of the lowest y layer of Ex (local slots and blocks received along x), [.., 1, :] of the highest, as rows of Ex, packed to the front, filled with 16; where 16 >= 8, some tile's list has no filler.
All inputs are finite; a program needn't handle non-finite values.
Results may differ from the reference program's by a relative error of at most 0.007.
Values may be sent and summed in bfloat16 or wider, within the bound.
No kernel may reach another device: no remote copies, remote signals or barrier semaphores. Data moves between devices by JAX's collectives and lax.ppermute only.
A program may use at most 128 MiB of HBM per device.

```python
import math
import jax
import jax.numpy as jnp
import numpy as np
from jax import lax

CHANNELS = 192
ACTION = 128
SLOTS = 16
TILE = 4
DEPTH = 2
VOXELS = 64
KERNEL = 27
FACE = 8
CROSS = 12
TILES_X = 16
TILES_Y = 32


def shift_grid(grid, axis_number, amount):
    length = grid.shape[axis_number]
    moved = jnp.roll(grid, amount, axis=axis_number)
    source = jnp.arange(length) - amount
    inside = (source >= 0) & (source < length)
    layout = [1] * grid.ndim
    layout[axis_number] = length
    return jnp.where(inside.reshape(layout), moved, -1)


def compact(candidates, length):
    empty = (candidates < 0).astype(jnp.int32)
    moved = jnp.argsort(empty, axis=-1, stable=True)
    packed = jnp.take_along_axis(candidates, moved, axis=-1)
    extent = candidates.shape[-1]
    if extent < length:
        filler = jnp.full(candidates.shape[:-1] + (length - extent,), -1, jnp.int32)
        packed = jnp.concatenate([packed, filler], axis=-1)
    packed = packed[..., :length]
    ranks = jnp.cumsum(1 - empty, axis=-1) - 1
    return (packed, ranks)


def scene(key):
    devices = TILES_X * TILES_Y
    places = TILE * TILE * DEPTH
    key_count, key_pick, key_place = jax.random.split(key, 3)
    key_row, key_column = jax.random.split(key_pick)
    lowest = max(2, SLOTS * 5 // 8)
    counts = jax.random.randint(key_count, (devices,), lowest, SLOTS + 1)
    pick_row = jax.random.randint(key_row, (), 1, TILES_X - 1)
    pick_column = jax.random.randint(key_column, (), 0, TILES_Y)
    fullest = pick_row * TILES_Y + pick_column
    second = pick_row * TILES_Y + (pick_column + 1) % TILES_Y
    tile_ids = jnp.arange(devices)
    counts = jnp.where((tile_ids == fullest) | (tile_ids == second), SLOTS, counts).astype(jnp.int32)
    place_index = np.arange(places)
    place_row = place_index // (TILE * DEPTH)
    place_column = place_index // DEPTH % TILE
    row_mask = jnp.asarray((place_column == 0).astype(np.int32))
    layer_mask = jnp.asarray((place_row == 0).astype(np.int32))
    corner_high = jnp.asarray(((place_row == TILE - 1) & (place_column == 0)).astype(np.int32))
    corner_low = jnp.asarray(((place_row == 0) & (place_column == 0)).astype(np.int32))
    forced = (tile_ids == fullest).astype(jnp.int32)[:, None] * row_mask + (tile_ids == second).astype(jnp.int32)[:, None] * layer_mask + (tile_ids == fullest - TILES_Y).astype(jnp.int32)[:, None] * corner_high + (tile_ids == fullest + TILES_Y).astype(jnp.int32)[:, None] * corner_low
    forced = jnp.minimum(forced, 1)
    place_keys = jax.random.split(key_place, devices)
    scores = jax.vmap(lambda single: jax.random.permutation(single, places))(place_keys).astype(jnp.int32)
    scores = scores + places * forced
    orders = jnp.argsort(-scores, axis=1, stable=True).astype(jnp.int32)
    ranks = jnp.argsort(orders, axis=1).astype(jnp.int32)
    slot_at = jnp.where(ranks < counts[:, None], ranks, -1).reshape(TILES_X, TILES_Y, TILE, TILE, DEPTH)
    face_low = slot_at[:, :, 0].reshape(TILES_X, TILES_Y, TILE * DEPTH)
    face_high = slot_at[:, :, TILE - 1].reshape(TILES_X, TILES_Y, TILE * DEPTH)
    list_low, rank_low = compact(face_low, FACE)
    list_high, rank_high = compact(face_high, FACE)
    send_x = jnp.stack([list_low, list_high], axis=2)
    send_x = jnp.where(send_x < 0, SLOTS, send_x)
    high_in = shift_grid(face_high, 0, 1)
    from_lower = jnp.where(high_in >= 0, SLOTS + 1 + jnp.roll(rank_high, 1, axis=0), -1)
    low_in = shift_grid(face_low, 0, -1)
    from_upper = jnp.where(low_in >= 0, SLOTS + 1 + FACE + jnp.roll(rank_low, -1, axis=0), -1)
    wide_map = jnp.concatenate([from_lower.reshape(TILES_X, TILES_Y, 1, TILE, DEPTH), slot_at, from_upper.reshape(TILES_X, TILES_Y, 1, TILE, DEPTH)], axis=2)
    cand_low = wide_map[:, :, :, 0].reshape(TILES_X, TILES_Y, (TILE + 2) * DEPTH)
    cand_high = wide_map[:, :, :, TILE - 1].reshape(TILES_X, TILES_Y, (TILE + 2) * DEPTH)
    cross_low, cross_rank_low = compact(cand_low, CROSS)
    cross_high, cross_rank_high = compact(cand_high, CROSS)
    send_y = jnp.stack([cross_low, cross_high], axis=2)
    send_y = jnp.where(send_y < 0, SLOTS, send_y)
    high_in_y = shift_grid(cand_high, 1, 1)
    below = jnp.where(high_in_y >= 0, SLOTS + 1 + 2 * FACE + jnp.roll(cross_rank_high, 1, axis=1), -1)
    below = below.reshape(TILES_X, TILES_Y, TILE + 2, 1, DEPTH)
    low_in_y = shift_grid(cand_low, 1, -1)
    above = jnp.where(low_in_y >= 0, SLOTS + 1 + 2 * FACE + CROSS + jnp.roll(cross_rank_low, -1, axis=1), -1)
    above = above.reshape(TILES_X, TILES_Y, TILE + 2, 1, DEPTH)
    full_map = jnp.concatenate([below, wide_map, above], axis=3)
    full_map = jnp.pad(full_map, ((0, 0), (0, 0), (0, 0), (0, 0), (1, 1)), constant_values=-1)
    positions = orders[:, :SLOTS]
    place_x = positions // (TILE * DEPTH)
    place_y = positions // DEPTH % TILE
    place_z = positions % DEPTH
    stride = np.arange(27)
    move_x = (stride // 9 - 1).astype(np.int32)
    move_y = (stride // 3 % 3 - 1).astype(np.int32)
    move_z = (stride % 3 - 1).astype(np.int32)
    target = ((place_x[:, :, None] + 1 + move_x) * (TILE + 2) + place_y[:, :, None] + 1 + move_y) * (DEPTH + 2) + place_z[:, :, None] + 1 + move_z
    flat_map = full_map.reshape(devices, -1)
    found = jnp.take_along_axis(flat_map, target.reshape(devices, -1).astype(jnp.int32), axis=1).reshape(devices, SLOTS, 27)
    used = jnp.arange(SLOTS)[None, :, None] < counts[:, None, None]
    neighbours = jnp.where(used & (found >= 0), found, SLOTS).astype(jnp.int32)
    return (counts.reshape(TILES_X, TILES_Y), neighbours.reshape(TILES_X, TILES_Y, SLOTS, 27), send_x.astype(jnp.int32), send_y.astype(jnp.int32))


def draw_counts(key, part):
    return scene(key)[0]


def draw_neighbours(key, part):
    return scene(key)[1]


def draw_send_x(key, part):
    return scene(key)[2]


def draw_send_y(key, part):
    return scene(key)[3]


def draw_features(key, part):
    key = jax.random.fold_in(key, 5)
    key_centre, key_rows, key_noise = jax.random.split(key, 3)
    devices = TILES_X * TILES_Y
    rising = 1.0 + 2.0 * jnp.arange(devices, dtype=jnp.float32) / max(devices - 1, 1)
    rising = rising.reshape(TILES_X, TILES_Y, 1, 1, 1)
    layout = (TILES_X, TILES_Y, SLOTS, VOXELS, CHANNELS)
    centre = 0.5 * jax.random.truncated_normal(key_centre, -4.0, 4.0, (1, 1, 1, 1, CHANNELS), jnp.float32)
    spread = jnp.exp(jax.random.uniform(key_rows, layout[:4] + (1,), jnp.float32, math.log(0.3), math.log(3.0)))
    noise = jax.random.truncated_normal(key_noise, -4.0, 4.0, layout, jnp.float32)
    return (rising * (centre + spread * noise)).astype(jnp.bfloat16)


def steps_of(rng, dims, shards, least, largest):
    gain, own = 1.0, jax.random.fold_in(rng, 6)
    for axis_at, shards_of in shards:
        draws = jnp.exp(jax.random.uniform(jax.random.fold_in(own, axis_at), (shards_of,), jnp.float32, least / len(shards), largest / len(shards)))
        gain = gain * jnp.repeat(draws, dims[axis_at] // shards_of).reshape([-1 if axis == axis_at else 1 for axis in range(len(dims))])
    return gain


def scatter_about(stream_key, shape, width, most, cuts=(), kind=jnp.bfloat16):
    drawn = width * jax.random.normal(stream_key, shape, jnp.float32)
    if cuts:
        drawn = drawn * steps_of(stream_key, shape, cuts, -0.22, 0.18)
    return jnp.clip(drawn, -most, most).astype(kind)


def setup_inputs(seed: int = 0) -> dict:
    key_of = jax.random.split(jax.random.key(seed), 10)
    features = draw_features(jax.random.fold_in(key_of[9], 71), 0)
    cotangent = scatter_about(key_of[1], (TILES_X, TILES_Y, SLOTS, VOXELS, CHANNELS), 1.0, 6.0, ((0, 16), (1, 32)))
    counts = draw_counts(jax.random.fold_in(key_of[9], 71), 0)
    neighbours = draw_neighbours(jax.random.fold_in(key_of[9], 71), 0)
    send_x = draw_send_x(jax.random.fold_in(key_of[9], 71), 0)
    send_y = draw_send_y(jax.random.fold_in(key_of[9], 71), 0)
    action = scatter_about(key_of[6], (ACTION,), 1.0, 6.0, (), jnp.float32)
    conv_weight = scatter_about(key_of[7], (CHANNELS, KERNEL, CHANNELS), (KERNEL * CHANNELS) ** -0.5, 0.078125)
    film_weight = scatter_about(key_of[8], (ACTION, 2 * CHANNELS), ACTION ** -0.5, 0.5, (), jnp.float32)
    return dict(features=features, cotangent=cotangent, counts=counts, neighbours=neighbours, send_x=send_x, send_y=send_y, action=action, conv_weight=conv_weight, film_weight=film_weight)


def offset_tables():
    block_table = np.zeros((64, 27), np.int32)
    voxel_table = np.zeros((64, 27), np.int32)
    for cell_index in range(64):
        position = [cell_index // 16, cell_index // 4 % 4, cell_index % 4]
        for offset_index in range(27):
            stride = [offset_index // 9 - 1, offset_index // 3 % 3 - 1, offset_index % 3 - 1]
            target = [position[axis_number] + stride[axis_number] for axis_number in range(3)]
            blocks = [(coordinate + 4) // 4 for coordinate in target]
            within = [(coordinate + 4) % 4 for coordinate in target]
            block_table[cell_index, offset_index] = (blocks[0] * 3 + blocks[1]) * 3 + blocks[2]
            voxel_table[cell_index, offset_index] = (within[0] * 4 + within[1]) * 4 + within[2]
    return (block_table, voxel_table)

def columns(extended, lookup):
    flat = extended.reshape(-1, extended.shape[-1])
    return flat[lookup].reshape(lookup.shape[0], -1)

def padded_tile(field, tile_row, tile_column):
    inside = (tile_row >= 0) & (tile_row < field.shape[0])
    safe_row = jnp.clip(tile_row, 0, field.shape[0] - 1)
    local = field[safe_row, tile_column]
    local = jnp.where(inside, local, jnp.zeros_like(local))
    zero_block = jnp.zeros((1,) + local.shape[1:], local.dtype)
    return (jnp.concatenate([local, zero_block], axis=0), safe_row)

def widened_tile(field, send_x, tile_row, tile_column):
    padded, unused_row = padded_tile(field, tile_row, tile_column)
    lower, lower_row = padded_tile(field, tile_row - 1, tile_column)
    upper, upper_row = padded_tile(field, tile_row + 1, tile_column)
    from_lower = lower[send_x[lower_row, tile_column, 1]]
    from_upper = upper[send_x[upper_row, tile_column, 0]]
    return jnp.concatenate([padded, from_lower, from_upper], axis=0)

def extended_tile(field, send_x, send_y, tile_row, tile_column):
    columns_y = field.shape[1]
    pieces = [widened_tile(field, send_x, tile_row, tile_column)]
    for offset_y, which_side in ((-1, 1), (1, 0)):
        other_column = tile_column + offset_y
        inside = (other_column >= 0) & (other_column < columns_y)
        safe_column = jnp.clip(other_column, 0, columns_y - 1)
        taken = widened_tile(field, send_x, tile_row, safe_column)[send_y[tile_row, safe_column, which_side]]
        pieces.append(jnp.where(inside, taken, jnp.zeros_like(taken)))
    return jnp.concatenate(pieces, axis=0)

def reference(features, cotangent, counts, neighbours, send_x, send_y, action, conv_weight, film_weight):
    block_table, voxel_table = offset_tables()
    grid_x, grid_y, slots, voxels, channels = features.shape
    live = (jnp.arange(slots)[None, None, :] < counts[:, :, None]).astype(jnp.float32)[..., None, None]
    inputs = features.astype(jnp.float32) * live
    cell_total = jnp.sum(counts).astype(jnp.float32) * voxels
    mean = lax.optimization_barrier(jnp.sum(inputs, axis=(0, 1, 2, 3))) / cell_total
    variance = lax.optimization_barrier(jnp.sum(inputs * inputs, axis=(0, 1, 2, 3))) / cell_total - mean * mean
    inverse = lax.rsqrt(variance + 1e-05)
    film = jnp.dot(action, film_weight, precision=lax.Precision.HIGHEST)
    scale = 1.0 + film[:channels]
    shift = film[channels:]
    hidden = (jnp.maximum((inputs - mean) * inverse * scale + shift, 0.0) * live).astype(jnp.bfloat16)
    upstream = cotangent * live.astype(jnp.bfloat16)
    weight_rows = conv_weight.reshape(channels, -1)
    flipped = jnp.transpose(conv_weight[:, ::-1, :], (1, 0, 2)).reshape(-1, channels)
    rows_total = slots * voxels

    def per_tile(carry, tile_number):
        weight_sum, shift_sum, scale_sum = carry
        tile_row = tile_number // grid_y
        tile_column = tile_number % grid_y
        lookup = (neighbours[tile_row, tile_column][:, block_table] * voxels + voxel_table).reshape(rows_total, -1)
        cols_hidden = columns(extended_tile(hidden, send_x, send_y, tile_row, tile_column), lookup)
        mixed = jnp.dot(cols_hidden, weight_rows.T, preferred_element_type=jnp.float32)
        tile_inputs = inputs[tile_row, tile_column]
        tile_live = live[tile_row, tile_column]
        tile_output = ((tile_inputs + mixed.reshape(slots, voxels, channels)) * tile_live).astype(jnp.bfloat16)
        cols_upstream = columns(extended_tile(upstream, send_x, send_y, tile_row, tile_column), lookup)
        back = jnp.dot(cols_upstream, flipped, preferred_element_type=jnp.float32).reshape(slots, voxels, channels)
        tile_upstream = upstream[tile_row, tile_column].reshape(rows_total, channels)
        weight_sum = weight_sum + jnp.dot(tile_upstream.T, cols_hidden, preferred_element_type=jnp.float32)
        normed = (tile_inputs - mean) * inverse
        active = (normed * scale + shift > 0).astype(jnp.float32) * tile_live
        slope = back * active
        shift_sum = shift_sum + lax.optimization_barrier(jnp.sum(slope, axis=(0, 1)))
        scale_sum = scale_sum + lax.optimization_barrier(jnp.sum(slope * normed, axis=(0, 1)))
        return ((weight_sum, shift_sum, scale_sum), (tile_output, slope))
    start = (jnp.zeros((channels, weight_rows.shape[1]), jnp.float32), jnp.zeros((channels,), jnp.float32), jnp.zeros((channels,), jnp.float32))
    (weight_sum, shift_grad, scale_grad), (outputs, slopes) = lax.scan(per_tile, start, jnp.arange(grid_x * grid_y, dtype=jnp.int32))
    output = outputs.reshape(features.shape)
    slope = slopes.reshape(features.shape)
    normed = (inputs - mean) * inverse
    grad_features = (upstream.astype(jnp.float32) + inverse * (slope * scale - scale * shift_grad / cell_total - normed * scale * scale_grad / cell_total)) * live
    grad_film = action[:, None] * jnp.concatenate([scale_grad, shift_grad])[None, :]
    return (output, grad_features.astype(jnp.bfloat16), weight_sum.reshape(conv_weight.shape), grad_film)
```

```python
import functools

import jax
import jax.numpy as jnp
from jax import lax
from jax.experimental import pallas as pl
from jax.experimental.pallas import tpu as pltpu
from jax.sharding import PartitionSpec as P

SLOTS = 16
VOXELS = 64
CHANNELS = 192
PAIRS = 14
VMEM_LIMIT = 56 * 1024 * 1024
F32 = jnp.float32
BF16 = jnp.bfloat16


def iota(shape, dim):
    return lax.broadcasted_iota(jnp.int32, shape, dim)


def dot(left, right):
    return jnp.dot(left, right, preferred_element_type=F32)


def dot_nt(left, right):
    return lax.dot_general(left, right, (((1,), (1,)), ((), ())), preferred_element_type=F32)


def swap_matrix(count):
    row, col = iota((256, 256), 0), iota((256, 256), 1)
    hit = ((row >> 4) == (col & 15)) & ((row & 15) == (col >> 4))
    if count is not None:
        hit = hit & ((row & 15) < count)
    return jnp.where(hit, 1.0, 0.0).astype(BF16)


def list_column(ref, side, length, rows, half):
    row = iota((rows, 1), 0)
    entry = jnp.full((rows, 1), -1, jnp.int32)
    for e in range(length):
        value = ref[side, e]
        entry = jnp.where((row == e) | (row == e + half), value, entry)
    return entry


def pick(column, width, low, high, base, second, half):
    rows = column.shape[0]
    row, col = iota((rows, width), 0), iota((rows, width), 1)
    target = column - low + base + jnp.where(row >= half, second, 0)
    hit = (column >= low) & (column < high) & (col == target)
    return jnp.where(hit, 1.0, 0.0).astype(BF16)


def pack_kernel(counts, send_x, feat, cot, action, film_weight, fields, stats, faces, film):
    count = counts[0]
    swap = swap_matrix(count)
    total = jnp.zeros((1, CHANNELS), F32)
    square = jnp.zeros((1, CHANNELS), F32)
    for g in range(4):
        part = slice(16 * g, 16 * g + 16)
        moved = dot(swap, feat[:, part, :].reshape(256, CHANNELS))
        total += jnp.sum(moved, axis=0, keepdims=True)
        square += jnp.sum(moved * moved, axis=0, keepdims=True)
        fields[part, 0:16, :] = moved.astype(BF16).reshape(16, 16, CHANNELS)
        moved = dot(swap, cot[:, part, :].reshape(256, CHANNELS))
        fields[part, 16:32, :] = moved.astype(BF16).reshape(16, 16, CHANNELS)
    row = iota((8, CHANNELS), 0)
    cells = (count * VOXELS).astype(F32)
    lines = jnp.where(row == 0, total, jnp.where(row == 1, square, jnp.where(row == 2, cells, 0.0)))
    for i in range(stats.shape[0]):
        stats[i, :, :] = lines
    for side in range(2):
        chosen = pick(list_column(send_x, side, 8, 16, 8), 32, 0, SLOTS, 0, 16, 8)
        for i in range(16):
            faces[side, i, :, :] = dot(chosen, fields[48 * side + i]).astype(BF16)
    film[...] = lax.dot_general(
        action[...],
        film_weight[...],
        (((1,), (0,)), ((), ())),
        precision=lax.Precision.HIGHEST,
        preferred_element_type=F32,
    )


def cross_kernel(send_y, fields, lower, upper, faces):
    for side in range(2):
        column = list_column(send_y, side, 12, 32, 16)
        local = pick(column, 32, 0, SLOTS, 0, 16, 16)
        from_lower = pick(column, 16, 17, 25, 0, 8, 16)
        from_upper = pick(column, 16, 25, 33, 0, 8, 16)
        for a in range(4):
            for c in range(4):
                value = dot(local, fields[16 * a + 12 * side + c])
                if a == 3:
                    value += dot(from_lower, lower[12 * side + c])
                if a == 0:
                    value += dot(from_upper, upper[12 * side + c])
                faces[side, 4 * a + c, :, :] = value.astype(BF16)


def norm_terms(stats, film):
    sums = jnp.sum(stats[...], axis=0)
    cells = sums[2:3, :]
    mean = sums[0:1, :] / cells
    variance = sums[1:2, :] / cells - mean * mean
    inverse = lax.rsqrt(variance + 1e-05)
    scale = 1.0 + film[:, :CHANNELS]
    shift = film[:, CHANNELS:]
    return cells, mean, inverse, scale, shift


def main_kernel(
    counts, fields, lower, upper, lower_y, upper_y, rule, stats, film, weight,
    output, gradients, kept, hid, low, high, low_y, high_y, padded, acc_m, acc_b, turned,
):
    count = counts[0]
    cells, mean, inverse, scale, shift = norm_terms(stats, film)

    def act(x):
        return jnp.maximum((x.astype(F32) - mean) * inverse * scale + shift, 0.0)

    live = iota((16, 1), 0) < count

    def local_part(i, carry):
        at = pl.ds(i * 16, 16)
        x = act(fields[at, 0:16, :].reshape(256, CHANNELS)).reshape(16, 16, CHANNELS)
        hid[at, 0:16, :] = jnp.where(live[None], x, 0.0).astype(BF16)
        hid[at, 16:32, :] = fields[at, 16:32, :]
        return carry

    lax.fori_loop(0, 4, local_part, 0)
    first_x = iota((256, 1), 0) % 16 < 8
    for source, target in ((lower, low), (upper, high)):
        x = source[...].reshape(256, CHANNELS)
        x = jnp.where(first_x, act(x), x.astype(F32))
        target[...] = x.astype(BF16).reshape(16, 16, CHANNELS)
    for source, target in ((lower_y, low_y), (upper_y, high_y)):
        x = act(source[:, 0:16, :].reshape(256, CHANNELS))
        target[:, 0:16, :] = x.astype(BF16).reshape(16, 16, CHANNELS)
        target[:, 16:32, :] = source[:, 16:32, :]

    entries = rule[...]
    row32 = iota((32, 128), 0)
    col32 = iota((32, 128), 1)
    second = row32 >= 16
    hot = []
    for n in range(27):
        column = entries[:, n : n + 1]
        column = jnp.concatenate([column, column], axis=0)
        target = jnp.where(second, column + 16, column)
        target = jnp.where(column >= 17, column + 15 + jnp.where(second, 8, 0), target)
        target = jnp.where(column >= 25, column + 23 + jnp.where(second, 8, 0), target)
        target = jnp.where(column >= 33, column + 31 + jnp.where(second, 16, 0), target)
        target = jnp.where(column >= 45, column + 51 + jnp.where(second, 16, 0), target)
        hit = (column != 16) & (col32 == target)
        hot.append(jnp.where(hit, 1.0, 0.0).astype(BF16))

    none16 = jnp.zeros((16, CHANNELS), BF16)
    none32 = jnp.zeros((32, CHANNELS), BF16)
    for a in range(4):
        for b in range(4):
            for c in range(4):
                own = hid[16 * a + 4 * b + c]
                padded[a + 1, b + 1, c + 1, :, :] = own
                ways = [
                    [(q + 1, 0)] + ([(5, 1)] if q == 0 else []) + ([(0, -1)] if q == 3 else [])
                    for q in (a, b, c)
                ]
                places = [(x, y, z) for x in ways[0] for y in ways[1] for z in ways[2]][1:]
                if not places:
                    continue
                listed = jnp.concatenate(
                    [
                        own,
                        low[4 * b + c] if a == 3 else none16,
                        high[4 * b + c] if a == 0 else none16,
                        low_y[4 * a + c] if b == 3 else none32,
                        high_y[4 * a + c] if b == 0 else none32,
                    ],
                    axis=0,
                )
                chosen = jnp.concatenate(
                    [hot[9 * (x[1] + 1) + 3 * (y[1] + 1) + z[1] + 1] for x, y, z in places], axis=0
                )
                found = dot(chosen, listed).astype(BF16)
                for m, (x, y, z) in enumerate(places):
                    padded[x[0], y[0], z[0], :, :] = found[32 * m : 32 * m + 32]

    row, col = iota((256, CHANNELS), 0), iota((256, CHANNELS), 1)
    spread = ((row & 15) < 12) & (col == (row >> 4) * 12 + (row & 15))
    spread = jnp.where(spread, 1.0, 0.0).astype(BF16)
    turned[...] = dot_nt(spread, fields[:, 16:32, :].reshape(1024, CHANNELS)).astype(BF16)

    acc_m[...] = jnp.zeros_like(acc_m)
    acc_b[...] = jnp.zeros_like(acc_b)

    def window(k, at):
        k = jnp.minimum(k, 26)
        x, y, z = k // 9, (k // 3) % 3, k % 3
        part = padded[pl.ds(x, 4), pl.ds(y, 4), pl.ds(z, 4), at, :]
        return part.reshape(1024, CHANNELS)

    def step(t, carry):
        k1, k2 = 2 * t, 2 * t + 1
        left1, left2 = window(k1, slice(0, 16)), window(k2, slice(0, 16))
        acc_m[...] += dot_nt(left1, weight[k1]) + dot_nt(left2, weight[k2])
        grad1 = dot(turned[...], left1)
        grad2 = dot(turned[...], left2)
        tail = jnp.concatenate([grad1[:, 128:], grad2[:, 128:]], axis=1)
        packed = jnp.concatenate([grad1[:, :128], grad2[:, :128], tail], axis=1)
        gradients[:, pl.ds(t, 1), :, :] = packed.astype(BF16).reshape(16, 1, 16, 384)
        up1, up2 = window(k1, slice(16, 32)), window(k2, slice(16, 32))
        back2 = jnp.where(k2 > 26, 27, 26 - k2)
        acc_b[...] += dot(up1, weight[26 - k1]) + dot(up2, weight[back2])
        return carry

    lax.fori_loop(0, PAIRS, step, 0)

    swap = swap_matrix(None)
    shift_grad = jnp.zeros((1, CHANNELS), F32)
    scale_grad = jnp.zeros((1, CHANNELS), F32)
    live256 = (iota((256, 1), 0) & 15) < count
    for g in range(4):
        at = slice(256 * g, 256 * g + 256)
        x = fields[16 * g : 16 * g + 16, 0:16, :].reshape(256, CHANNELS).astype(F32)
        mixed = jnp.where(live256, x + acc_m[at, :], 0.0).astype(BF16)
        output[:, 16 * g : 16 * g + 16, :] = dot(swap, mixed).astype(BF16).reshape(16, 16, CHANNELS)
        normed = (x - mean) * inverse
        slope = jnp.where(live256 & (normed * scale + shift > 0), acc_b[at, :], 0.0)
        shift_grad += jnp.sum(slope, axis=0, keepdims=True)
        scale_grad += jnp.sum(slope * normed, axis=0, keepdims=True)
        up = fields[16 * g : 16 * g + 16, 16:32, :].reshape(256, CHANNELS).astype(F32)
        kept[at, :] = up + inverse * (slope * scale)
    sums = jnp.concatenate([scale_grad, shift_grad], axis=1)
    first = sums.astype(BF16).astype(F32)
    rest = sums - first
    second_part = rest.astype(BF16).astype(F32)
    row = iota((16, 384), 0)
    lines = jnp.where(
        row == 12, first, jnp.where(row == 13, second_part, jnp.where(row == 14, rest - second_part, 0.0))
    )
    held = gradients[:, 0, :, :].astype(F32)
    gradients[:, 0, :, :] = jnp.where((row < 12)[None], held, lines[None]).astype(BF16)


def share_kernel(parts, shares):
    for t in range(PAIRS):
        total = jnp.sum(parts[:, t, :, :].astype(F32), axis=0)
        if t == 0:
            sums = total[12:13] + total[13:14] + total[14:15]
            first = sums.astype(BF16).astype(F32)
            rest = sums - first
            second = rest.astype(BF16).astype(F32)
            third = rest - second
        for m in range(3):
            share, place = divmod(3 * t + m, 2)
            shares[share, place, :, :] = total[:, 128 * m : 128 * m + 128].astype(BF16)
    for tile in range(3 * PAIRS, 64):
        share, place = divmod(tile, 2)
        shares[share, place, :, :] = jnp.zeros((16, 128), BF16)
    row = iota((16, 128), 0)
    lines = jnp.zeros((16, 128), F32)
    for e, piece in enumerate((first, second, third)):
        for m in range(3):
            lines = jnp.where(row == 3 * e + m, piece[:, 128 * m : 128 * m + 128], lines)
    for share in range(32):
        shares[share, 2, :, :] = lines.astype(BF16)


def finish_kernel(counts, parts, stats, film, action, fields, kept, mine, grad_film, grad_inputs):
    total = jnp.sum(parts[...].astype(F32), axis=0)
    for i in range(32):
        mine[i, :, :, :] = total[0:2].astype(BF16)
    tile = total[2]
    line = tile[0:3] + tile[3:6] + tile[6:9]
    sums = jnp.concatenate([line[0:1], line[1:2], line[2:3]], axis=1)
    scale_grad, shift_grad = sums[:, :CHANNELS], sums[:, CHANNELS:]
    cells, mean, inverse, scale, shift = norm_terms(stats, film)
    grad_film[...] = action[...] * sums
    swap = swap_matrix(None)
    live = (iota((256, 1), 0) & 15) < counts[0]
    for g in range(4):
        x = fields[16 * g : 16 * g + 16, 0:16, :].reshape(256, CHANNELS).astype(F32)
        normed = (x - mean) * inverse
        value = kept[256 * g : 256 * g + 256, :] - inverse * (
            scale * shift_grad / cells + normed * scale * scale_grad / cells
        )
        value = jnp.where(live, value, 0.0).astype(BF16)
        value = dot(swap, value).astype(BF16).reshape(16, 16, CHANNELS)
        grad_inputs[:, 16 * g : 16 * g + 16, :] = value


SMEM = pl.BlockSpec(memory_space=pltpu.SMEM)
VMEM = pl.BlockSpec(memory_space=pltpu.VMEM)


def call(kernel, specs, outs, scratch=(), flops=0, name=None):
    shapes = [jax.ShapeDtypeStruct(shape, dtype) for shape, dtype in outs]
    moved = sum(int(jnp.dtype(d).itemsize) * functools.reduce(int.__mul__, s) for s, d in outs)
    return pl.pallas_call(
        kernel,
        out_shape=shapes,
        in_specs=specs,
        out_specs=[VMEM] * len(outs),
        scratch_shapes=list(scratch),
        compiler_params=pltpu.CompilerParams(vmem_limit_bytes=VMEM_LIMIT),
        cost_estimate=pl.CostEstimate(flops=flops, bytes_accessed=2 * moved, transcendentals=0),
        name=name,
    )


def exchange(array, axis):
    return lax.all_to_all(array, axis, 0, 0, tiled=True)


def body(features, cotangent, counts, neighbours, send_x, send_y, action, conv_weight, film_weight):
    size_x, size_y = lax.axis_size("gx"), lax.axis_size("gy")
    count = counts.reshape(1)
    fields, stats, faces, film = call(
        pack_kernel,
        [SMEM, SMEM, VMEM, VMEM, VMEM, VMEM],
        [
            ((VOXELS, 32, CHANNELS), BF16),
            ((size_x, 8, CHANNELS), F32),
            ((2, 16, 16, CHANNELS), BF16),
            ((1, 2 * CHANNELS), F32),
        ],
        flops=10**9,
        name="pack",
    )(count, send_x[0, 0], features[0, 0], cotangent[0, 0], action[None], film_weight)
    up_x = [(i, i + 1) for i in range(size_x - 1)]
    down_x = [(i + 1, i) for i in range(size_x - 1)]
    up_y = [(i, i + 1) for i in range(size_y - 1)]
    down_y = [(i + 1, i) for i in range(size_y - 1)]
    lower = lax.ppermute(faces[1], "gx", up_x)
    upper = lax.ppermute(faces[0], "gx", down_x)
    stats = jnp.sum(exchange(stats, "gx"), axis=0)
    weight = jnp.pad(jnp.transpose(conv_weight, (1, 0, 2)), ((0, 1), (0, 0), (0, 0)))
    (cross,) = call(
        cross_kernel, [SMEM, VMEM, VMEM, VMEM], [((2, 16, 32, CHANNELS), BF16)], flops=10**8, name="cross"
    )(send_y[0, 0], fields, lower, upper)
    lower_y = lax.ppermute(cross[1], "gy", up_y)
    upper_y = lax.ppermute(cross[0], "gy", down_y)
    stats = exchange(jnp.broadcast_to(stats[None], (size_y,) + stats.shape), "gy")
    output, gradients, kept = call(
        main_kernel,
        [SMEM] + [VMEM] * 9,
        [
            ((SLOTS, VOXELS, CHANNELS), BF16),
            ((16, PAIRS, 16, 384), BF16),
            ((1024, CHANNELS), F32),
        ],
        [
            pltpu.VMEM((VOXELS, 32, CHANNELS), BF16),
            pltpu.VMEM((16, 16, CHANNELS), BF16),
            pltpu.VMEM((16, 16, CHANNELS), BF16),
            pltpu.VMEM((16, 32, CHANNELS), BF16),
            pltpu.VMEM((16, 32, CHANNELS), BF16),
            pltpu.VMEM((6, 6, 6, 32, CHANNELS), BF16),
            pltpu.VMEM((1024, CHANNELS), F32),
            pltpu.VMEM((1024, CHANNELS), F32),
            pltpu.VMEM((256, 1024), BF16),
        ],
        flops=10**10,
        name="convolve",
    )(count, fields, lower, upper, lower_y, upper_y, neighbours[0, 0], stats, film, weight)
    gradients = exchange(gradients, "gx")
    (shares,) = call(
        share_kernel, [VMEM], [((32, 3, 16, 128), BF16)], flops=10**6, name="share"
    )(gradients)
    shares = exchange(shares, "gy")
    mine, grad_film, grad_inputs = call(
        finish_kernel,
        [SMEM] + [VMEM] * 6,
        [
            ((32, 2, 16, 128), BF16),
            ((128, 2 * CHANNELS), F32),
            ((SLOTS, VOXELS, CHANNELS), BF16),
        ],
        flops=10**9,
        name="finish",
    )(count, shares, stats, film, action[:, None], fields, kept)
    tiles = exchange(mine, "gy").reshape(64, 16, 128)[: 3 * PAIRS]
    tiles = tiles.reshape(PAIRS, 3, 16, 128)[:, :, :12].astype(F32)
    even = jnp.concatenate([tiles[:, 0], tiles[:, 2, :, :64]], axis=-1)
    odd = jnp.concatenate([tiles[:, 1], tiles[:, 2, :, 64:]], axis=-1)
    grad_weight = jnp.stack([even, odd], axis=1).reshape(28, 12, CHANNELS)[:27].transpose(1, 0, 2)
    return output[None, None], grad_inputs[None, None], grad_weight, grad_film


def solution(mesh):
    tile = P("gx", "gy")
    return jax.shard_map(
        body,
        mesh=mesh,
        in_specs=(tile, tile, tile, tile, tile, tile, P(), P(), P()),
        out_specs=(tile, tile, P("gx"), P()),
        check_vma=False,
    )
```

```python
import jax
import jax.numpy as jnp
from jax import lax
from jax.experimental import pallas as pl
from jax.experimental.pallas import tpu as pltpu
from jax.sharding import PartitionSpec as P

SLOTS = 16
VOXELS = 64
CHANNELS = 192
TILES = 11
VMEM_LIMIT = 56 * 1024 * 1024
F32 = jnp.float32
BF16 = jnp.bfloat16


def iota(shape, dim):
    return lax.broadcasted_iota(jnp.int32, shape, dim)


def dot(left, right):
    return jnp.dot(left, right, preferred_element_type=F32)


def dot_nt(left, right):
    return lax.dot_general(left, right, (((1,), (1,)), ((), ())), preferred_element_type=F32)


def swap_matrix(count):
    row, col = iota((256, 256), 0), iota((256, 256), 1)
    hit = ((row >> 4) == (col & 15)) & ((row & 15) == (col >> 4))
    if count is not None:
        hit = hit & ((row & 15) < count)
    return jnp.where(hit, 1.0, 0.0).astype(BF16)


def list_column(ref, side, length, rows, half):
    row = iota((rows, 1), 0)
    entry = jnp.full((rows, 1), -1, jnp.int32)
    for e in range(length):
        value = ref[side, e]
        entry = jnp.where((row == e) | (row == e + half), value, entry)
    return entry


def pick(column, width, low, high, base, second, half):
    rows = column.shape[0]
    row, col = iota((rows, width), 0), iota((rows, width), 1)
    target = column - low + base + jnp.where(row >= half, second, 0)
    hit = (column >= low) & (column < high) & (col == target)
    return jnp.where(hit, 1.0, 0.0).astype(BF16)


def pack_lines(first, second):
    rest = jnp.concatenate([first[:, 128:], second[:, 128:]], axis=1)
    return [first[:, :128], second[:, :128], rest]


def unpack_lines(lines):
    first = jnp.concatenate([lines[0:1], lines[2:3, :64]], axis=1)
    second = jnp.concatenate([lines[1:2], lines[2:3, 64:]], axis=1)
    return first, second


def stack_lines(lines, rows):
    row = iota((rows, 128), 0)
    block = jnp.zeros((rows, 128), F32)
    for e, line in enumerate(lines):
        block = jnp.where(row == e, line, block)
    return block


def pack_kernel(counts, send_x, feat, cot, action, film_weight, held, up, stats, faces, film):
    count = counts[0]
    swap = swap_matrix(count)
    total = jnp.zeros((1, CHANNELS), F32)
    square = jnp.zeros((1, CHANNELS), F32)
    for g in range(4):
        part = slice(16 * g, 16 * g + 16)
        moved = dot(swap, feat[:, part, :].reshape(256, CHANNELS))
        total += jnp.sum(moved, axis=0, keepdims=True)
        square += jnp.sum(moved * moved, axis=0, keepdims=True)
        held[part, :, :] = moved.astype(BF16).reshape(16, 16, CHANNELS)
        moved = dot(swap, cot[:, part, :].reshape(256, CHANNELS))
        up[part, :, :] = moved.astype(BF16).reshape(16, 16, CHANNELS)
    cells = (count * VOXELS).astype(F32)
    block = stack_lines(pack_lines(total, square) + [cells], 4)
    for i in range(stats.shape[0]):
        stats[i, :, :] = block
    for side in range(2):
        chosen = pick(list_column(send_x, side, 8, 16, 8), 32, 0, SLOTS, 0, 16, 8)
        for i in range(16):
            both = jnp.concatenate([held[48 * side + i], up[48 * side + i]], axis=0)
            faces[side, i, :, :] = dot(chosen, both).astype(BF16)
    film[...] = lax.dot_general(
        action[...],
        film_weight[...],
        (((1,), (0,)), ((), ())),
        precision=lax.Precision.HIGHEST,
        preferred_element_type=F32,
    )


def cross_kernel(send_y, held, up, lower, upper, stats, faces, up_faces, spread):
    block = jnp.sum(stats[...], axis=0)
    for i in range(spread.shape[0]):
        spread[i, :, :] = block
    for side in range(2):
        column = list_column(send_y, side, 12, 32, 16)
        local = pick(column, 32, 0, SLOTS, 0, 16, 16)
        from_lower = pick(column, 16, 17, 25, 0, 8, 16)
        from_upper = pick(column, 16, 25, 33, 0, 8, 16)
        for a in range(4):
            for c in range(4):
                v = 16 * a + 12 * side + c
                value = dot(local, jnp.concatenate([held[v], up[v]], axis=0))
                if a == 3:
                    value += dot(from_lower, lower[12 * side + c])
                if a == 0:
                    value += dot(from_upper, upper[12 * side + c])
                value = value.astype(BF16)
                faces[side, 4 * a + c, :, :] = value[0:16]
                up_faces[side, 4 * a + c, :, :] = value[16:32]


def norm_terms(stats, film):
    lines = jnp.sum(stats[...], axis=0)
    total, square = unpack_lines(lines)
    cells = lines[3:4, 0:1]
    mean = total / cells
    variance = square / cells - mean * mean
    inverse = lax.rsqrt(variance + 1e-05)
    scale = 1.0 + film[:, :CHANNELS]
    shift = film[:, CHANNELS:]
    return cells, mean, inverse, scale, shift


def gather_blocks(rule, half, own, low, high, low_y, high_y, padded):
    entries = rule[...]
    col = iota((16, 80), 1)
    hot = []
    for n in range(27):
        column = entries[:, n : n + 1]
        target = jnp.where(column >= 17, column - 1 + half, column)
        target = jnp.where(column >= 25, column + 7 + half, target)
        target = jnp.where(column >= 33, column + 15, target)
        target = jnp.where(column >= 45, column + 19, target)
        hit = (column != 16) & (col == target)
        hot.append(jnp.where(hit, 1.0, 0.0).astype(BF16))
    none = jnp.zeros((16, CHANNELS), BF16)
    for a in range(4):
        for b in range(4):
            for c in range(4):
                mine = own[16 * a + 4 * b + c]
                padded[a + 1, b + 1, c + 1, :, :] = mine
                ways = [
                    [(q + 1, 0)] + ([(5, 1)] if q == 0 else []) + ([(0, -1)] if q == 3 else [])
                    for q in (a, b, c)
                ]
                places = [(x, y, z) for x in ways[0] for y in ways[1] for z in ways[2]][1:]
                if not places:
                    continue
                listed = jnp.concatenate(
                    [
                        mine,
                        low[4 * b + c] if a == 3 else none,
                        high[4 * b + c] if a == 0 else none,
                        low_y[4 * a + c] if b == 3 else none,
                        high_y[4 * a + c] if b == 0 else none,
                    ],
                    axis=0,
                )
                chosen = jnp.concatenate(
                    [hot[9 * (x[1] + 1) + 3 * (y[1] + 1) + z[1] + 1] for x, y, z in places], axis=0
                )
                found = dot(chosen, listed).astype(BF16)
                for m, (x, y, z) in enumerate(places):
                    padded[x[0], y[0], z[0], :, :] = found[16 * m : 16 * m + 16]


def window(padded, k):
    x, y, z = k // 9, (k // 3) % 3, k % 3
    part = padded[pl.ds(x, 4), pl.ds(y, 4), pl.ds(z, 4), :, :]
    return part.reshape(1024, CHANNELS)


def weight_kernel(
    counts, held, up, lower, upper, lower_y, upper_y, rule, stats, film,
    gradients, padded, hid, low, high, low_y, high_y, turned,
):
    cells, mean, inverse, scale, shift = norm_terms(stats, film)

    def act(x):
        x = (x.astype(F32) - mean) * inverse * scale + shift
        return jnp.maximum(x, 0.0).astype(BF16)

    live = (iota((256, 1), 0) & 15) < counts[0]

    def local_part(i, carry):
        at = pl.ds(i * 16, 16)
        x = act(held[at, :, :].reshape(256, CHANNELS))
        x = jnp.where(live, x.astype(F32), 0.0).astype(BF16)
        hid[at, :, :] = x.reshape(16, 16, CHANNELS)
        return carry

    lax.fori_loop(0, 4, local_part, 0)
    for source, target in ((lower, low), (upper, high), (lower_y, low_y), (upper_y, high_y)):
        target[...] = act(source[...].reshape(256, CHANNELS)).reshape(16, 16, CHANNELS)
    gather_blocks(rule, 0, hid, low, high, low_y, high_y, padded)

    row, col = iota((256, CHANNELS), 0), iota((256, CHANNELS), 1)
    group = row >> 4
    wide = up[...].reshape(1024, CHANNELS)
    for m in range(4):
        place = (row + 4 * m) & 15
        spread = (place < 12) & (col == group * 12 + place)
        spread = jnp.where(spread, 1.0, 0.0).astype(BF16)
        turned[m, :, :] = dot_nt(spread, wide).astype(BF16)

    line = iota((256, 384), 0) & 15

    def pair(m, k1, k2):
        grad1 = dot(turned[m], window(padded, k1))
        grad2 = dot(turned[m], window(padded, k2)) if k2 is not None else jnp.zeros_like(grad1)
        rest = jnp.concatenate([grad1[:, 128:], grad2[:, 128:]], axis=1)
        return jnp.concatenate([grad1[:, :128], grad2[:, :128], rest], axis=1)

    def store(at, value):
        gradients[:, pl.ds(at, 1), :, :] = value.astype(BF16).reshape(16, 1, 16, 384)

    def step(q, carry):
        k = 8 * q
        first, second = pair(0, k, k + 1), pair(1, k + 2, k + 3)
        store(3 * q, jnp.where(line < 12, first, second))
        third = pair(2, k + 4, k + 5)
        store(3 * q + 1, jnp.where(line < 8, second, third))
        fourth = pair(3, k + 6, k + 7)
        store(3 * q + 2, jnp.where(line < 4, third, fourth))
        return carry

    lax.fori_loop(0, 3, step, 0)
    first, second = pair(0, 24, 25), pair(1, 26, None)
    store(9, jnp.where(line < 12, first, second))
    store(10, jnp.where(line < 8, second, 0.0))


def field_kernel(
    counts, held, up, lower, upper, lower_y, upper_y, rule, stats, film, weight, padded,
    output, kept, sums, wide, acc_m, acc_b,
):
    count = counts[0]
    cells, mean, inverse, scale, shift = norm_terms(stats, film)
    gather_blocks(rule, 8, up, lower, upper, lower_y, upper_y, wide)
    acc_m[...] = jnp.zeros_like(acc_m)
    acc_b[...] = jnp.zeros_like(acc_b)

    def step(t, carry):
        k = 3 * t
        total = dot_nt(window(padded, k), weight[k])
        total += dot_nt(window(padded, k + 1), weight[k + 1])
        acc_m[...] += total + dot_nt(window(padded, k + 2), weight[k + 2])
        total = dot(window(wide, k), weight[26 - k])
        total += dot(window(wide, k + 1), weight[25 - k])
        acc_b[...] += total + dot(window(wide, k + 2), weight[24 - k])
        return carry

    lax.fori_loop(0, 9, step, 0)

    swap = swap_matrix(None)
    shift_grad = jnp.zeros((1, CHANNELS), F32)
    scale_grad = jnp.zeros((1, CHANNELS), F32)
    live = (iota((256, 1), 0) & 15) < count
    for g in range(4):
        at = slice(256 * g, 256 * g + 256)
        part = slice(16 * g, 16 * g + 16)
        x = held[part, :, :].reshape(256, CHANNELS).astype(F32)
        mixed = jnp.where(live, x + acc_m[at, :], 0.0).astype(BF16)
        output[:, part, :] = dot(swap, mixed).astype(BF16).reshape(16, 16, CHANNELS)
        normed = (x - mean) * inverse
        slope = jnp.where(live & (normed * scale + shift > 0), acc_b[at, :], 0.0)
        shift_grad += jnp.sum(slope, axis=0, keepdims=True)
        scale_grad += jnp.sum(slope * normed, axis=0, keepdims=True)
        kept[at, :] = up[part, :, :].reshape(256, CHANNELS).astype(F32) + inverse * (slope * scale)
    block = stack_lines(pack_lines(scale_grad, shift_grad), 4)
    sums[...] = block


def place_of(share):
    return (share // 3, share % 3) if share < 30 else (10, 2 * (share - 30))


def share_kernel(parts, sums, shares):
    lines = jnp.sum(sums[...], axis=0)
    first = lines.astype(BF16).astype(F32)
    second = lines - first
    block = stack_lines([first[e : e + 1] for e in range(3)] + [second[e : e + 1] for e in range(3)], 8)
    for tile in range(TILES):
        total = jnp.sum(parts[:, tile, :, :].astype(F32), axis=0)
        for share in range(32):
            if place_of(share)[0] == tile:
                third = place_of(share)[1]
                mine = total[:, 128 * third : 128 * third + 128]
                shares[share, :, :] = jnp.concatenate([mine, block], axis=0).astype(BF16)


def own_kernel(parts, mine, sums):
    total = jnp.sum(parts[...].astype(F32), axis=0)
    for i in range(mine.shape[0]):
        mine[i, :, :] = total[0:16].astype(BF16)
    sums[...] = total[16:24]


def finish_kernel(counts, sums, stats, film, action, held, kept, grad_film, grad_inputs):
    lines = sums[0:3, :] + sums[3:6, :]
    scale_grad, shift_grad = unpack_lines(lines)
    cells, mean, inverse, scale, shift = norm_terms(stats, film)
    grad_film[:, :CHANNELS] = action[...] * scale_grad
    grad_film[:, CHANNELS:] = action[...] * shift_grad
    swap = swap_matrix(None)
    live = (iota((256, 1), 0) & 15) < counts[0]
    for g in range(4):
        part = slice(16 * g, 16 * g + 16)
        x = held[part, :, :].reshape(256, CHANNELS).astype(F32)
        normed = (x - mean) * inverse
        value = kept[256 * g : 256 * g + 256, :] - inverse * (
            scale * shift_grad / cells + normed * scale * scale_grad / cells
        )
        value = jnp.where(live, value, 0.0).astype(BF16)
        grad_inputs[:, part, :] = dot(swap, value).astype(BF16).reshape(16, 16, CHANNELS)


def unpack_kernel(tiles, grad_weight):
    zero = jnp.zeros((16, 128), BF16)
    thirds = [
        jnp.concatenate([tiles[3 * u + n] for u in range(10)] + [last], axis=0)
        for n, last in enumerate((tiles[30], zero, tiles[31]))
    ]
    even = jnp.concatenate([thirds[0], thirds[2][:, :64]], axis=1)
    odd = jnp.concatenate([thirds[1], thirds[2][:, 64:]], axis=1)
    row, col = iota((384, 352), 0), iota((384, 352), 1)
    k = row & 31
    chosen = (k < 27) & (col == (row >> 5) + 12 * (k >> 1) + 176 * (k & 1))
    chosen = jnp.where(chosen, 1.0, 0.0).astype(BF16)
    found = dot(chosen, jnp.concatenate([even, odd], axis=0)).reshape(12, 32, CHANNELS)
    grad_weight[...] = found[:, :27, :]


SMEM = pl.BlockSpec(memory_space=pltpu.SMEM)
VMEM = pl.BlockSpec(memory_space=pltpu.VMEM)


def call(kernel, scalars, arrays, outs, scratch=(), flops=0, name=None):
    shapes = [jax.ShapeDtypeStruct(shape, dtype) for shape, dtype in outs]
    moved = sum(x.size * x.dtype.itemsize for x in [*arrays, *shapes])
    return pl.pallas_call(
        kernel,
        out_shape=shapes,
        in_specs=[SMEM] * len(scalars) + [VMEM] * len(arrays),
        out_specs=[VMEM] * len(outs),
        scratch_shapes=[pltpu.VMEM(*s) for s in scratch],
        compiler_params=pltpu.CompilerParams(vmem_limit_bytes=VMEM_LIMIT),
        cost_estimate=pl.CostEstimate(flops=flops, bytes_accessed=moved, transcendentals=0),
        name=name,
    )(*scalars, *arrays)


def exchange(array, axis):
    return lax.all_to_all(array, axis, 0, 0, tiled=True)


def body(features, cotangent, counts, neighbours, send_x, send_y, action, conv_weight, film_weight):
    size_x, size_y = lax.axis_size("gx"), lax.axis_size("gy")
    count = counts.reshape(1)
    rule = neighbours[0, 0]
    block = ((VOXELS, 16, CHANNELS), BF16)
    face = ((16, 16, CHANNELS), BF16)
    spaced = ((6, 6, 6, 16, CHANNELS), BF16)
    held, up, stats, faces, film = call(
        pack_kernel,
        [count, send_x[0, 0]],
        [features[0, 0], cotangent[0, 0], action[None], film_weight],
        [block, block, ((size_x, 4, 128), F32), ((2, *face[0]), BF16), ((1, 2 * CHANNELS), F32)],
        flops=10**9,
        name="pack",
    )
    up_x = [(i, i + 1) for i in range(size_x - 1)]
    down_x = [(i + 1, i) for i in range(size_x - 1)]
    up_y = [(i, i + 1) for i in range(size_y - 1)]
    down_y = [(i + 1, i) for i in range(size_y - 1)]
    lower = lax.ppermute(faces[1], "gx", up_x)
    upper = lax.ppermute(faces[0], "gx", down_x)
    stats = exchange(stats, "gx")
    weight = jnp.transpose(conv_weight, (1, 0, 2))
    cross, cross_up, stats = call(
        cross_kernel,
        [send_y[0, 0]],
        [held, up, lower, upper, stats],
        [((2, *face[0]), BF16), ((2, *face[0]), BF16), ((size_y, 4, 128), F32)],
        flops=10**8,
        name="cross",
    )
    lower_y = lax.ppermute(cross[1], "gy", up_y)
    upper_y = lax.ppermute(cross[0], "gy", down_y)
    lower_u = lax.ppermute(cross_up[1], "gy", up_y)
    upper_u = lax.ppermute(cross_up[0], "gy", down_y)
    stats = exchange(stats, "gy")
    gradients, padded = call(
        weight_kernel,
        [count],
        [held, up, lower, upper, lower_y, upper_y, rule, stats, film],
        [((16, TILES, 16, 384), BF16), spaced],
        [block, face, face, face, face, ((4, 256, 1024), BF16)],
        flops=4 * 10**9,
        name="weight",
    )
    gradients = exchange(gradients, "gx")
    output, kept, sums = call(
        field_kernel,
        [count],
        [held, up, lower, upper, lower_u, upper_u, rule, stats, film, weight, padded],
        [((SLOTS, VOXELS, CHANNELS), BF16), ((1024, CHANNELS), F32), ((4, 128), F32)],
        [spaced, ((1024, CHANNELS), F32), ((1024, CHANNELS), F32)],
        flops=6 * 10**9,
        name="field",
    )
    sums = lax.all_gather(sums, "gx")
    (shares,) = call(share_kernel, [], [gradients, sums], [((size_y, 24, 128), BF16)], name="share")
    shares = exchange(shares, "gy")
    mine, sums = call(
        own_kernel, [], [shares], [((size_y, 16, 128), BF16), ((8, 128), F32)], name="own"
    )
    tiles = exchange(mine, "gy")
    grad_film, grad_inputs = call(
        finish_kernel,
        [count],
        [sums, stats, film, action[:, None], held, kept],
        [((128, 2 * CHANNELS), F32), ((SLOTS, VOXELS, CHANNELS), BF16)],
        flops=10**9,
        name="finish",
    )
    (grad_weight,) = call(unpack_kernel, [], [tiles], [((12, 27, CHANNELS), F32)], name="unpack")
    return output[None, None], grad_inputs[None, None], grad_weight, grad_film


def solution(mesh):
    tile = P("gx", "gy")
    return jax.shard_map(
        body,
        mesh=mesh,
        in_specs=(tile, tile, tile, tile, tile, tile, P(), P(), P()),
        out_specs=(tile, tile, P("gx"), P()),
        check_vma=False,
    )
```

```python
import jax
import jax.numpy as jnp
from jax import lax
from jax.experimental import pallas as pl
from jax.experimental.pallas import tpu as pltpu
from jax.sharding import PartitionSpec as P

SLOTS = 16
VOXELS = 64
CHANNELS = 192
TILES = 11
VMEM_LIMIT = 56 * 1024 * 1024
F32 = jnp.float32
BF16 = jnp.bfloat16


def iota(shape, dim):
    return lax.broadcasted_iota(jnp.int32, shape, dim)


def dot(left, right):
    return jnp.dot(left, right, preferred_element_type=F32)


def dot_nt(left, right):
    return lax.dot_general(left, right, (((1,), (1,)), ((), ())), preferred_element_type=F32)


def swap_matrix(count):
    row, col = iota((256, 256), 0), iota((256, 256), 1)
    hit = ((row >> 4) == (col & 15)) & ((row & 15) == (col >> 4))
    if count is not None:
        hit = hit & ((row & 15) < count)
    return jnp.where(hit, 1.0, 0.0).astype(BF16)


def list_column(ref, side, length, rows, half):
    row = iota((rows, 1), 0)
    entry = jnp.full((rows, 1), -1, jnp.int32)
    for e in range(length):
        value = ref[side, e]
        entry = jnp.where((row == e) | (row == e + half), value, entry)
    return entry


def pick(column, width, low, high, base, second, half):
    rows = column.shape[0]
    row, col = iota((rows, width), 0), iota((rows, width), 1)
    target = column - low + base + jnp.where(row >= half, second, 0)
    hit = (column >= low) & (column < high) & (col == target)
    return jnp.where(hit, 1.0, 0.0).astype(BF16)


def pack_lines(first, second):
    rest = jnp.concatenate([first[:, 128:], second[:, 128:]], axis=1)
    return [first[:, :128], second[:, :128], rest]


def unpack_lines(lines):
    first = jnp.concatenate([lines[0:1], lines[2:3, :64]], axis=1)
    second = jnp.concatenate([lines[1:2], lines[2:3, 64:]], axis=1)
    return first, second


def stack_lines(lines, rows):
    row = iota((rows, 128), 0)
    block = jnp.zeros((rows, 128), F32)
    for e, line in enumerate(lines):
        block = jnp.where(row == e, line, block)
    return block


def join_fields(value):
    first, second = value[0:16], value[16:32]
    rest = jnp.concatenate([first[:, 128:], second[:, 128:]], axis=1)
    return jnp.concatenate([first[:, :128], second[:, :128], rest], axis=1).astype(BF16)


def one_field(joined, which):
    tail = joined[..., 256:320] if which == 0 else joined[..., 320:384]
    return jnp.concatenate([joined[..., 128 * which : 128 * which + 128], tail], axis=-1)


def pack_kernel(
    counts, send_x, send_y, feat, cot, action, film_weight, held, up, stats, faces, sides, film
):
    count = counts[0]
    swap = swap_matrix(count)
    total = jnp.zeros((1, CHANNELS), F32)
    square = jnp.zeros((1, CHANNELS), F32)
    for g in range(4):
        part = slice(16 * g, 16 * g + 16)
        moved = dot(swap, feat[:, part, :].reshape(256, CHANNELS))
        total += jnp.sum(moved, axis=0, keepdims=True)
        square += jnp.sum(moved * moved, axis=0, keepdims=True)
        held[part, :, :] = moved.astype(BF16).reshape(16, 16, CHANNELS)
        moved = dot(swap, cot[:, part, :].reshape(256, CHANNELS))
        up[part, :, :] = moved.astype(BF16).reshape(16, 16, CHANNELS)
    cells = (count * VOXELS).astype(F32)
    block = stack_lines(pack_lines(total, square) + [cells], 4)
    for i in range(stats.shape[0]):
        stats[i, :, :] = block
    for side in range(2):
        chosen = pick(list_column(send_x, side, 8, 16, 8), 32, 0, SLOTS, 0, 16, 8)
        for i in range(16):
            both = jnp.concatenate([held[48 * side + i], up[48 * side + i]], axis=0)
            faces[side, i, :, :] = dot(chosen, both).astype(BF16)
    for side in range(2):
        chosen = pick(list_column(send_y, side, 12, 32, 16), 32, 0, SLOTS, 0, 16, 16)
        for a in range(4):
            for c in range(4):
                v = 16 * a + 12 * side + c
                both = jnp.concatenate([held[v], up[v]], axis=0)
                sides[side, 4 * a + c, :, :] = join_fields(dot(chosen, both))
    film[...] = lax.dot_general(
        action[...],
        film_weight[...],
        (((1,), (0,)), ((), ())),
        precision=lax.Precision.HIGHEST,
        preferred_element_type=F32,
    )


def cross_kernel(send_y, lower, upper, stats, corners, spread):
    block = jnp.sum(stats[...], axis=0)
    for i in range(spread.shape[0]):
        spread[i, :, :] = block
    for side in range(2):
        column = list_column(send_y, side, 12, 32, 16)
        from_lower = pick(column, 16, 17, 25, 0, 8, 16)
        from_upper = pick(column, 16, 25, 33, 0, 8, 16)
        for c in range(4):
            corners[side, c, :, :] = join_fields(dot(from_upper, upper[12 * side + c]))
            corners[side, 4 + c, :, :] = join_fields(dot(from_lower, lower[12 * side + c]))


def beside_y(side, corner, which):
    part = one_field(side[...], which).astype(F32)
    more = one_field(corner[...], which).astype(F32)
    return jnp.concatenate([part[0:4] + more[0:4], part[4:12], part[12:16] + more[4:8]], axis=0)


def norm_terms(stats, film):
    lines = jnp.sum(stats[...], axis=0)
    total, square = unpack_lines(lines)
    cells = lines[3:4, 0:1]
    mean = total / cells
    variance = square / cells - mean * mean
    inverse = lax.rsqrt(variance + 1e-05)
    scale = 1.0 + film[:, :CHANNELS]
    shift = film[:, CHANNELS:]
    return cells, mean, inverse, scale, shift


def gather_blocks(rule, half, own, low, high, low_y, high_y, padded):
    entries = rule[...]
    col = iota((16, 80), 1)
    hot = []
    for n in range(27):
        column = entries[:, n : n + 1]
        target = jnp.where(column >= 17, column - 1 + half, column)
        target = jnp.where(column >= 25, column + 7 + half, target)
        target = jnp.where(column >= 33, column + 15, target)
        target = jnp.where(column >= 45, column + 19, target)
        hit = (column != 16) & (col == target)
        hot.append(jnp.where(hit, 1.0, 0.0).astype(BF16))
    none = jnp.zeros((16, CHANNELS), BF16)
    for a in range(4):
        for b in range(4):
            for c in range(4):
                mine = own[16 * a + 4 * b + c]
                padded[a + 1, b + 1, c + 1, :, :] = mine
                ways = [
                    [(q + 1, 0)] + ([(5, 1)] if q == 0 else []) + ([(0, -1)] if q == 3 else [])
                    for q in (a, b, c)
                ]
                places = [(x, y, z) for x in ways[0] for y in ways[1] for z in ways[2]][1:]
                if not places:
                    continue
                listed = jnp.concatenate(
                    [
                        mine,
                        low[4 * b + c] if a == 3 else none,
                        high[4 * b + c] if a == 0 else none,
                        low_y[4 * a + c] if b == 3 else none,
                        high_y[4 * a + c] if b == 0 else none,
                    ],
                    axis=0,
                )
                chosen = jnp.concatenate(
                    [hot[9 * (x[1] + 1) + 3 * (y[1] + 1) + z[1] + 1] for x, y, z in places], axis=0
                )
                found = dot(chosen, listed).astype(BF16)
                for m, (x, y, z) in enumerate(places):
                    padded[x[0], y[0], z[0], :, :] = found[16 * m : 16 * m + 16]


def window(padded, k):
    x, y, z = k // 9, (k // 3) % 3, k % 3
    part = padded[pl.ds(x, 4), pl.ds(y, 4), pl.ds(z, 4), :, :]
    return part.reshape(1024, CHANNELS)


def weight_kernel(
    counts, held, up, lower, upper, side_l, side_u, corner_l, corner_u, rule, stats, film,
    gradients, padded, hid, low, high, low_y, high_y, turned,
):
    cells, mean, inverse, scale, shift = norm_terms(stats, film)

    def act(x):
        x = (x.astype(F32) - mean) * inverse * scale + shift
        return jnp.maximum(x, 0.0).astype(BF16)

    live = (iota((256, 1), 0) & 15) < counts[0]

    def local_part(i, carry):
        at = pl.ds(i * 16, 16)
        x = act(held[at, :, :].reshape(256, CHANNELS))
        x = jnp.where(live, x.astype(F32), 0.0).astype(BF16)
        hid[at, :, :] = x.reshape(16, 16, CHANNELS)
        return carry

    lax.fori_loop(0, 4, local_part, 0)
    for source, target in (
        (lower[...], low),
        (upper[...], high),
        (beside_y(side_l, corner_l, 0), low_y),
        (beside_y(side_u, corner_u, 0), high_y),
    ):
        target[...] = act(source.reshape(256, CHANNELS)).reshape(16, 16, CHANNELS)
    gather_blocks(rule, 0, hid, low, high, low_y, high_y, padded)

    row, col = iota((256, CHANNELS), 0), iota((256, CHANNELS), 1)
    group = row >> 4
    wide = up[...].reshape(1024, CHANNELS)
    for m in range(4):
        place = (row + 4 * m) & 15
        spread = (place < 12) & (col == group * 12 + place)
        spread = jnp.where(spread, 1.0, 0.0).astype(BF16)
        turned[m, :, :] = dot_nt(spread, wide).astype(BF16)

    line = iota((256, 384), 0) & 15

    def pair(m, k1, k2):
        grad1 = dot(turned[m], window(padded, k1))
        grad2 = dot(turned[m], window(padded, k2)) if k2 is not None else jnp.zeros_like(grad1)
        rest = jnp.concatenate([grad1[:, 128:], grad2[:, 128:]], axis=1)
        return jnp.concatenate([grad1[:, :128], grad2[:, :128], rest], axis=1)

    def store(at, value):
        gradients[:, pl.ds(at, 1), :, :] = value.astype(BF16).reshape(16, 1, 16, 384)

    def step(q, carry):
        k = 8 * q
        first, second = pair(0, k, k + 1), pair(1, k + 2, k + 3)
        store(3 * q, jnp.where(line < 12, first, second))
        third = pair(2, k + 4, k + 5)
        store(3 * q + 1, jnp.where(line < 8, second, third))
        fourth = pair(3, k + 6, k + 7)
        store(3 * q + 2, jnp.where(line < 4, third, fourth))
        return carry

    lax.fori_loop(0, 3, step, 0)
    first, second = pair(0, 24, 25), pair(1, 26, None)
    store(9, jnp.where(line < 12, first, second))
    store(10, jnp.where(line < 8, second, 0.0))


def field_kernel(
    counts, held, up, lower, upper, side_l, side_u, corner_l, corner_u, rule, stats, film,
    weight_at, padded_at, output, kept, sums, wide, acc_m, acc_b, low_y, high_y, weight, padded, done,
):
    copies = [
        pltpu.make_async_copy(weight_at, weight, done.at[0]),
        pltpu.make_async_copy(padded_at, padded, done.at[1]),
    ]
    for copy in copies:
        copy.start()
    count = counts[0]
    cells, mean, inverse, scale, shift = norm_terms(stats, film)
    low_y[...] = beside_y(side_l, corner_l, 1).astype(BF16)
    high_y[...] = beside_y(side_u, corner_u, 1).astype(BF16)
    gather_blocks(rule, 8, up, lower, upper, low_y, high_y, wide)
    for copy in copies:
        copy.wait()
    acc_m[...] = jnp.zeros_like(acc_m)
    acc_b[...] = jnp.zeros_like(acc_b)

    def step(t, carry):
        k = 3 * t
        total = dot_nt(window(padded, k), weight[k])
        total += dot_nt(window(padded, k + 1), weight[k + 1])
        acc_m[...] += total + dot_nt(window(padded, k + 2), weight[k + 2])
        total = dot(window(wide, k), weight[26 - k])
        total += dot(window(wide, k + 1), weight[25 - k])
        acc_b[...] += total + dot(window(wide, k + 2), weight[24 - k])
        return carry

    lax.fori_loop(0, 9, step, 0)

    swap = swap_matrix(None)
    shift_grad = jnp.zeros((1, CHANNELS), F32)
    scale_grad = jnp.zeros((1, CHANNELS), F32)
    live = (iota((256, 1), 0) & 15) < count
    for g in range(4):
        at = slice(256 * g, 256 * g + 256)
        part = slice(16 * g, 16 * g + 16)
        x = held[part, :, :].reshape(256, CHANNELS).astype(F32)
        mixed = jnp.where(live, x + acc_m[at, :], 0.0).astype(BF16)
        output[:, part, :] = dot(swap, mixed).astype(BF16).reshape(16, 16, CHANNELS)
        normed = (x - mean) * inverse
        slope = jnp.where(live & (normed * scale + shift > 0), acc_b[at, :], 0.0)
        shift_grad += jnp.sum(slope, axis=0, keepdims=True)
        scale_grad += jnp.sum(slope * normed, axis=0, keepdims=True)
        kept[at, :] = up[part, :, :].reshape(256, CHANNELS).astype(F32) + inverse * (slope * scale)
    block = stack_lines(pack_lines(scale_grad, shift_grad), 4)
    sums[...] = block


def place_of(share):
    return (share // 3, share % 3) if share < 30 else (10, 2 * (share - 30))


def share_kernel(parts, sums, shares):
    lines = jnp.sum(sums[...], axis=0)
    first = lines.astype(BF16).astype(F32)
    second = lines - first
    block = stack_lines([first[e : e + 1] for e in range(3)] + [second[e : e + 1] for e in range(3)], 8)
    for tile in range(TILES):
        total = jnp.sum(parts[:, tile, :, :].astype(F32), axis=0)
        for share in range(32):
            if place_of(share)[0] == tile:
                third = place_of(share)[1]
                mine = total[:, 128 * third : 128 * third + 128]
                shares[share, :, :] = jnp.concatenate([mine, block], axis=0).astype(BF16)


def own_kernel(parts, mine, sums):
    total = jnp.sum(parts[...].astype(F32), axis=0)
    for i in range(mine.shape[0]):
        mine[i, :, :] = total[0:16].astype(BF16)
    sums[...] = total[16:24]


def finish_kernel(counts, sums, stats, film, action, held, kept, grad_film, grad_inputs):
    lines = sums[0:3, :] + sums[3:6, :]
    scale_grad, shift_grad = unpack_lines(lines)
    cells, mean, inverse, scale, shift = norm_terms(stats, film)
    grad_film[:, :CHANNELS] = action[...] * scale_grad
    grad_film[:, CHANNELS:] = action[...] * shift_grad
    swap = swap_matrix(None)
    live = (iota((256, 1), 0) & 15) < counts[0]
    for g in range(4):
        part = slice(16 * g, 16 * g + 16)
        x = held[part, :, :].reshape(256, CHANNELS).astype(F32)
        normed = (x - mean) * inverse
        value = kept[256 * g : 256 * g + 256, :] - inverse * (
            scale * shift_grad / cells + normed * scale * scale_grad / cells
        )
        value = jnp.where(live, value, 0.0).astype(BF16)
        grad_inputs[:, part, :] = dot(swap, value).astype(BF16).reshape(16, 16, CHANNELS)


def unpack_kernel(tiles, grad_weight):
    zero = jnp.zeros((16, 128), BF16)
    thirds = [
        jnp.concatenate([tiles[3 * u + n] for u in range(10)] + [last], axis=0)
        for n, last in enumerate((tiles[30], zero, tiles[31]))
    ]
    even = jnp.concatenate([thirds[0], thirds[2][:, :64]], axis=1)
    odd = jnp.concatenate([thirds[1], thirds[2][:, 64:]], axis=1)
    row, col = iota((384, 352), 0), iota((384, 352), 1)
    k = row & 31
    chosen = (k < 27) & (col == (row >> 5) + 12 * (k >> 1) + 176 * (k & 1))
    chosen = jnp.where(chosen, 1.0, 0.0).astype(BF16)
    found = dot(chosen, jnp.concatenate([even, odd], axis=0)).reshape(12, 32, CHANNELS)
    grad_weight[...] = found[:, :27, :]


SMEM = pl.BlockSpec(memory_space=pltpu.SMEM)
VMEM = pl.BlockSpec(memory_space=pltpu.VMEM)
ANY = pl.BlockSpec(memory_space=pl.ANY)


def call(kernel, scalars, arrays, outs, scratch=(), flops=0, name=None, left=0):
    shapes = [jax.ShapeDtypeStruct(shape, dtype) for shape, dtype in outs]
    moved = sum(x.size * x.dtype.itemsize for x in [*arrays, *shapes])
    return pl.pallas_call(
        kernel,
        out_shape=shapes,
        in_specs=[SMEM] * len(scalars) + [VMEM] * (len(arrays) - left) + [ANY] * left,
        out_specs=[VMEM] * len(outs),
        scratch_shapes=[pltpu.VMEM(*s) for s in scratch]
        + ([pltpu.SemaphoreType.DMA((left,))] if left else []),
        compiler_params=pltpu.CompilerParams(vmem_limit_bytes=VMEM_LIMIT),
        cost_estimate=pl.CostEstimate(flops=flops, bytes_accessed=moved, transcendentals=0),
        name=name,
    )(*scalars, *arrays)


def exchange(array, axis):
    return lax.all_to_all(array, axis, 0, 0, tiled=True)


def body(features, cotangent, counts, neighbours, send_x, send_y, action, conv_weight, film_weight):
    size_x, size_y = lax.axis_size("gx"), lax.axis_size("gy")
    count = counts.reshape(1)
    rule = neighbours[0, 0]
    block = ((VOXELS, 16, CHANNELS), BF16)
    face = ((16, 16, CHANNELS), BF16)
    spaced = ((6, 6, 6, 16, CHANNELS), BF16)
    joined = ((2, 16, 16, 384), BF16)
    held, up, stats, faces, sides, film = call(
        pack_kernel,
        [count, send_x[0, 0], send_y[0, 0]],
        [features[0, 0], cotangent[0, 0], action[None], film_weight],
        [block, block, ((size_y, 4, 128), F32), ((2, *face[0]), BF16), joined, ((1, 2 * CHANNELS), F32)],
        flops=10**9,
        name="pack",
    )
    up_x = [(i, i + 1) for i in range(size_x - 1)]
    down_x = [(i + 1, i) for i in range(size_x - 1)]
    up_y = [(i, i + 1) for i in range(size_y - 1)]
    down_y = [(i + 1, i) for i in range(size_y - 1)]
    lower = lax.ppermute(faces[1], "gx", up_x)
    upper = lax.ppermute(faces[0], "gx", down_x)
    side_l = lax.ppermute(sides[1], "gy", up_y)
    side_u = lax.ppermute(sides[0], "gy", down_y)
    stats = exchange(stats, "gy")
    weight = jnp.transpose(conv_weight, (1, 0, 2))
    corners, stats = call(
        cross_kernel,
        [send_y[0, 0]],
        [lower, upper, stats],
        [((2, 8, 16, 384), BF16), ((size_x, 4, 128), F32)],
        flops=10**8,
        name="cross",
    )
    corner_l = lax.ppermute(corners[1], "gy", up_y)
    corner_u = lax.ppermute(corners[0], "gy", down_y)
    stats = exchange(stats, "gx")
    gradients, padded = call(
        weight_kernel,
        [count],
        [held, up, lower, upper, side_l, side_u, corner_l, corner_u, rule, stats, film],
        [((16, TILES, 16, 384), BF16), spaced],
        [block, face, face, face, face, ((4, 256, 1024), BF16)],
        flops=4 * 10**9,
        name="weight",
    )
    gradients = exchange(gradients, "gx")
    output, kept, sums = call(
        field_kernel,
        [count],
        [held, up, lower, upper, side_l, side_u, corner_l, corner_u, rule, stats, film, weight, padded],
        [((SLOTS, VOXELS, CHANNELS), BF16), ((1024, CHANNELS), F32), ((4, 128), F32)],
        [spaced, ((1024, CHANNELS), F32), ((1024, CHANNELS), F32), face, face, ((27, 192, 192), BF16), spaced],
        flops=6 * 10**9,
        name="field",
        left=2,
    )
    sums = lax.all_gather(sums, "gx")
    (shares,) = call(share_kernel, [], [gradients, sums], [((size_y, 24, 128), BF16)], name="share")
    shares = exchange(shares, "gy")
    mine, sums = call(
        own_kernel, [], [shares], [((size_y, 16, 128), BF16), ((8, 128), F32)], name="own"
    )
    tiles = exchange(mine, "gy")
    grad_film, grad_inputs = call(
        finish_kernel,
        [count],
        [sums, stats, film, action[:, None], held, kept],
        [((128, 2 * CHANNELS), F32), ((SLOTS, VOXELS, CHANNELS), BF16)],
        flops=10**9,
        name="finish",
    )
    (grad_weight,) = call(unpack_kernel, [], [tiles], [((12, 27, CHANNELS), F32)], name="unpack")
    return output[None, None], grad_inputs[None, None], grad_weight, grad_film


def solution(mesh):
    tile = P("gx", "gy")
    return jax.shard_map(
        body,
        mesh=mesh,
        in_specs=(tile, tile, tile, tile, tile, tile, P(), P(), P()),
        out_specs=(tile, tile, P("gx"), P()),
        check_vma=False,
    )
```

```python
import jax
import jax.numpy as jnp
from jax import lax
from jax.experimental import pallas as pl
from jax.experimental.pallas import tpu as pltpu
from jax.sharding import PartitionSpec as P

SLOTS = 16
VOXELS = 64
CHANNELS = 192
TILES = 11
VMEM_LIMIT = 56 * 1024 * 1024
F32 = jnp.float32
BF16 = jnp.bfloat16


def iota(shape, dim):
    return lax.broadcasted_iota(jnp.int32, shape, dim)


def dot(left, right):
    return jnp.dot(left, right, preferred_element_type=F32)


def dot_nt(left, right):
    return lax.dot_general(left, right, (((1,), (1,)), ((), ())), preferred_element_type=F32)


def swap_matrix(count):
    row, col = iota((256, 256), 0), iota((256, 256), 1)
    hit = ((row >> 4) == (col & 15)) & ((row & 15) == (col >> 4))
    if count is not None:
        hit = hit & ((row & 15) < count)
    return jnp.where(hit, 1.0, 0.0).astype(BF16)


def list_column(ref, side, length, rows, half):
    row = iota((rows, 1), 0)
    entry = jnp.full((rows, 1), -1, jnp.int32)
    for e in range(length):
        value = ref[side, e]
        entry = jnp.where((row == e) | (row == e + half), value, entry)
    return entry


def pick(column, width, low, high, base, second, half):
    rows = column.shape[0]
    row, col = iota((rows, width), 0), iota((rows, width), 1)
    target = column - low + base + jnp.where(row >= half, second, 0)
    hit = (column >= low) & (column < high) & (col == target)
    return jnp.where(hit, 1.0, 0.0).astype(BF16)


def pack_lines(first, second):
    rest = jnp.concatenate([first[:, 128:], second[:, 128:]], axis=1)
    return [first[:, :128], second[:, :128], rest]


def unpack_lines(lines):
    first = jnp.concatenate([lines[0:1], lines[2:3, :64]], axis=1)
    second = jnp.concatenate([lines[1:2], lines[2:3, 64:]], axis=1)
    return first, second


def stack_lines(lines, rows):
    row = iota((rows, 128), 0)
    block = jnp.zeros((rows, 128), F32)
    for e, line in enumerate(lines):
        block = jnp.where(row == e, line, block)
    return block


def join_fields(value):
    first, second = value[0:16], value[16:32]
    rest = jnp.concatenate([first[:, 128:], second[:, 128:]], axis=1)
    return jnp.concatenate([first[:, :128], second[:, :128], rest], axis=1).astype(BF16)


def one_field(joined, which):
    tail = joined[..., 256:320] if which == 0 else joined[..., 320:384]
    return jnp.concatenate([joined[..., 128 * which : 128 * which + 128], tail], axis=-1)


def pack_kernel(
    counts, send_x, feat, cot, action, film_weight, held, up, stats, faces, film
):
    swap = swap_matrix(counts[0])
    total = jnp.zeros((1, CHANNELS), F32)
    square = jnp.zeros((1, CHANNELS), F32)
    for g in range(4):
        part = slice(16 * g, 16 * g + 16)
        moved = dot(swap, feat[:, part, :].reshape(256, CHANNELS))
        total += jnp.sum(moved, axis=0, keepdims=True)
        square += jnp.sum(moved * moved, axis=0, keepdims=True)
        held[part, :, :] = moved.astype(BF16).reshape(16, 16, CHANNELS)
        moved = dot(swap, cot[:, part, :].reshape(256, CHANNELS))
        up[part, :, :] = moved.astype(BF16).reshape(16, 16, CHANNELS)
    cells = (counts[0] * VOXELS).astype(F32)
    block = stack_lines(pack_lines(total, square) + [cells], 4)
    for i in range(stats.shape[0]):
        stats[i, :, :] = block
    for side in range(2):
        chosen = pick(list_column(send_x, side, 8, 16, 8), 32, 0, SLOTS, 0, 16, 8)
        for i in range(16):
            both = jnp.concatenate([held[48 * side + i], up[48 * side + i]], axis=0)
            faces[side, i, :, :] = dot(chosen, both).astype(BF16)
    film[...] = lax.dot_general(
        action[...],
        film_weight[...],
        (((1,), (0,)), ((), ())),
        precision=lax.Precision.HIGHEST,
        preferred_element_type=F32,
    )


def cross_kernel(send_y, held, up, lower, upper, stats, face_low, face_high, spread):
    block = jnp.sum(stats[...], axis=0)
    for i in range(spread.shape[0]):
        spread[i, :, :] = block
    for side in range(2):
        target = (face_low, face_high)[side]
        column = list_column(send_y, side, 12, 32, 16)
        local = pick(column, 32, 0, SLOTS, 0, 16, 16)
        from_lower = pick(column, 16, 17, 25, 0, 8, 16)
        from_upper = pick(column, 16, 25, 33, 0, 8, 16)
        for a in range(4):
            for c in range(4):
                v = 16 * a + 12 * side + c
                value = dot(local, jnp.concatenate([held[v], up[v]], axis=0))
                if a == 3:
                    value += dot(from_lower, lower[12 * side + c])
                if a == 0:
                    value += dot(from_upper, upper[12 * side + c])
                target[4 * a + c, :, :] = join_fields(value)


def norm_terms(stats, film):
    lines = jnp.sum(stats[...], axis=0)
    total, square = unpack_lines(lines)
    cells = lines[3:4, 0:1]
    mean = total / cells
    variance = square / cells - mean * mean
    inverse = lax.rsqrt(variance + 1e-05)
    scale = 1.0 + film[:, :CHANNELS]
    shift = film[:, CHANNELS:]
    return cells, mean, inverse, scale, shift


def gather_blocks(rule, half, own, low, high, low_y, high_y, padded):
    entries = rule[...]
    col = iota((16, 80), 1)
    hot = []
    for n in range(27):
        column = entries[:, n : n + 1]
        target = jnp.where(column >= 17, column - 1 + half, column)
        target = jnp.where(column >= 25, column + 7 + half, target)
        target = jnp.where(column >= 33, column + 15, target)
        target = jnp.where(column >= 45, column + 19, target)
        hit = (column != 16) & (col == target)
        hot.append(jnp.where(hit, 1.0, 0.0).astype(BF16))
    none = jnp.zeros((16, CHANNELS), BF16)
    for a in range(4):
        for b in range(4):
            for c in range(4):
                mine = own[16 * a + 4 * b + c]
                padded[a + 1, b + 1, c + 1, :, :] = mine
                ways = [
                    [(q + 1, 0)] + ([(5, 1)] if q == 0 else []) + ([(0, -1)] if q == 3 else [])
                    for q in (a, b, c)
                ]
                places = [(x, y, z) for x in ways[0] for y in ways[1] for z in ways[2]][1:]
                if not places:
                    continue
                listed = jnp.concatenate(
                    [
                        mine,
                        low[4 * b + c] if a == 3 else none,
                        high[4 * b + c] if a == 0 else none,
                        low_y[4 * a + c] if b == 3 else none,
                        high_y[4 * a + c] if b == 0 else none,
                    ],
                    axis=0,
                )
                chosen = jnp.concatenate(
                    [hot[9 * (x[1] + 1) + 3 * (y[1] + 1) + z[1] + 1] for x, y, z in places], axis=0
                )
                found = dot(chosen, listed).astype(BF16)
                for m, (x, y, z) in enumerate(places):
                    padded[x[0], y[0], z[0], :, :] = found[16 * m : 16 * m + 16]


def window(padded, k):
    x, y, z = k // 9, (k // 3) % 3, k % 3
    part = padded[pl.ds(x, 4), pl.ds(y, 4), pl.ds(z, 4), :, :]
    return part.reshape(1024, CHANNELS)


def weight_kernel(
    counts, core, held, up, lower, upper, side_l, side_u, rule, stats, film,
    near, far, padded, hid, low, high, low_y, high_y, turned,
):
    cells, mean, inverse, scale, shift = norm_terms(stats, film)

    def act(x):
        x = (x.astype(F32) - mean) * inverse * scale + shift
        return jnp.maximum(x, 0.0).astype(BF16)

    live = (iota((256, 1), 0) & 15) < counts[0]

    def local_part(i, carry):
        at = pl.ds(i * 16, 16)
        x = act(held[at, :, :].reshape(256, CHANNELS))
        x = jnp.where(live, x.astype(F32), 0.0).astype(BF16)
        hid[at, :, :] = x.reshape(16, 16, CHANNELS)
        return carry

    lax.fori_loop(0, 4, local_part, 0)
    for source, target in (
        (lower[...], low),
        (upper[...], high),
        (one_field(side_l[...], 0), low_y),
        (one_field(side_u[...], 0), high_y),
    ):
        target[...] = act(source.reshape(256, CHANNELS)).reshape(16, 16, CHANNELS)
    gather_blocks(rule, 0, hid, low, high, low_y, high_y, padded)

    row, col = iota((256, CHANNELS), 0), iota((256, CHANNELS), 1)
    group = ((row >> 4) & 7) * 2 + jnp.where(row >= 128, 1 - core[0], core[0])
    wide = up[...].reshape(1024, CHANNELS)
    for m in range(4):
        place = (row + 4 * m) & 15
        spread = (place < 12) & (col == group * 12 + place)
        spread = jnp.where(spread, 1.0, 0.0).astype(BF16)
        turned[m, :, :] = dot_nt(spread, wide).astype(BF16)

    line = iota((256, 384), 0) & 15

    def pair(m, k1, k2):
        grad1 = dot(turned[m], window(padded, k1))
        grad2 = dot(turned[m], window(padded, k2)) if k2 is not None else jnp.zeros_like(grad1)
        rest = jnp.concatenate([grad1[:, 128:], grad2[:, 128:]], axis=1)
        return jnp.concatenate([grad1[:, :128], grad2[:, :128], rest], axis=1)

    def store(at, value):
        value = value.astype(BF16).reshape(16, 1, 16, 384)
        near[:, pl.ds(at, 1), :, :] = value[:8]
        far[:, pl.ds(at, 1), :, :] = value[8:]

    def step(q, carry):
        k = 8 * q
        first, second = pair(0, k, k + 1), pair(1, k + 2, k + 3)
        store(3 * q, jnp.where(line < 12, first, second))
        third = pair(2, k + 4, k + 5)
        store(3 * q + 1, jnp.where(line < 8, second, third))
        fourth = pair(3, k + 6, k + 7)
        store(3 * q + 2, jnp.where(line < 4, third, fourth))
        return carry

    lax.fori_loop(0, 3, step, 0)
    first, second = pair(0, 24, 25), pair(1, 26, None)
    store(9, jnp.where(line < 12, first, second))
    store(10, jnp.where(line < 8, second, 0.0))


def back_kernel(
    counts, held, up, lower, upper, side_l, side_u, rule, stats, film,
    weight_at, kept, sums, wide, acc, low_y, high_y, weight, done,
):
    copy = pltpu.make_async_copy(weight_at, weight, done.at[0])
    copy.start()
    cells, mean, inverse, scale, shift = norm_terms(stats, film)
    low_y[...] = one_field(side_l[...], 1)
    high_y[...] = one_field(side_u[...], 1)
    gather_blocks(rule, 8, up, lower, upper, low_y, high_y, wide)
    acc[...] = jnp.zeros_like(acc)
    copy.wait()

    def step(t, carry):
        k = 3 * t
        total = dot(window(wide, k), weight[26 - k])
        total += dot(window(wide, k + 1), weight[25 - k])
        acc[...] += total + dot(window(wide, k + 2), weight[24 - k])
        return carry

    lax.fori_loop(0, 9, step, 0)
    shift_grad = jnp.zeros((1, CHANNELS), F32)
    scale_grad = jnp.zeros((1, CHANNELS), F32)
    live = (iota((256, 1), 0) & 15) < counts[0]
    for g in range(4):
        at = slice(256 * g, 256 * g + 256)
        part = slice(16 * g, 16 * g + 16)
        x = held[part, :, :].reshape(256, CHANNELS).astype(F32)
        normed = (x - mean) * inverse
        slope = jnp.where(live & (normed * scale + shift > 0), acc[at, :], 0.0)
        shift_grad += jnp.sum(slope, axis=0, keepdims=True)
        scale_grad += jnp.sum(slope * normed, axis=0, keepdims=True)
        kept[at, :] = up[part, :, :].reshape(256, CHANNELS).astype(F32) + inverse * (slope * scale)
    sums[...] = jnp.concatenate([scale_grad, shift_grad], axis=1)


def split(value):
    first = value.astype(BF16).astype(F32)
    second = (value - first).astype(BF16).astype(F32)
    return first, second, value - first - second


def combine_kernel(near, other, sums, parts):
    for i in range(8):
        parts[i, :, :, :] = (near[i].astype(F32) + other[i].astype(F32)).astype(BF16)
    row = iota((16, 384), 0)
    lines = jnp.zeros((16, 384), F32)
    for e, piece in enumerate(split(sums[...])):
        lines = jnp.where(row == 8 + e, piece, lines)
    for i in range(8):
        held = parts[i, TILES - 1, :, :].astype(F32)
        parts[i, TILES - 1, :, :] = jnp.where(row < 8, held, lines).astype(BF16)


def forward_kernel(
    counts, held, weight_at, padded_at, output, acc, weight, padded, done
):
    copies = [
        pltpu.make_async_copy(weight_at, weight, done.at[0]),
        pltpu.make_async_copy(padded_at, padded, done.at[1]),
    ]
    for copy in copies:
        copy.start()
    acc[...] = jnp.zeros_like(acc)
    for copy in copies:
        copy.wait()

    def step(t, carry):
        k = 3 * t
        total = dot_nt(window(padded, k), weight[k])
        total += dot_nt(window(padded, k + 1), weight[k + 1])
        acc[...] += total + dot_nt(window(padded, k + 2), weight[k + 2])
        return carry

    lax.fori_loop(0, 9, step, 0)
    swap = swap_matrix(None)
    live = (iota((256, 1), 0) & 15) < counts[0]
    for g in range(4):
        part = slice(16 * g, 16 * g + 16)
        x = held[part, :, :].reshape(256, CHANNELS).astype(F32)
        mixed = jnp.where(live, x + acc[256 * g : 256 * g + 256, :], 0.0).astype(BF16)
        output[:, part, :] = dot(swap, mixed).astype(BF16).reshape(16, 16, CHANNELS)


def place_of(share):
    return (share // 3, share % 3) if share < 30 else (10, 2 * (share - 30))


def share_kernel(parts, output, shares):
    for tile in reversed(range(TILES)):
        total = jnp.sum(parts[:, tile, :, :].astype(F32), axis=0)
        if tile == TILES - 1:
            sums = total[8:9] + total[9:10] + total[10:11]
            pieces = split(sums)[:2]
            lines = [piece[:, 128 * m : 128 * m + 128] for piece in pieces for m in range(3)]
            block = stack_lines(lines, 8)
        for share in range(32):
            if place_of(share)[0] == tile:
                third = place_of(share)[1]
                mine = total[:, 128 * third : 128 * third + 128]
                shares[share, :, :] = jnp.concatenate([mine, block], axis=0).astype(BF16)


def own_kernel(parts, mine, sums):
    total = jnp.sum(parts[...].astype(F32), axis=0)
    for i in range(mine.shape[0]):
        mine[i, :, :] = total[0:16].astype(BF16)
    lines = total[16:19] + total[19:22]
    sums[...] = jnp.concatenate([lines[0:1], lines[1:2], lines[2:3]], axis=1)


def finish_kernel(counts, sums, other, stats, film, action, held, kept, grad_film, grad_inputs):
    total = sums[...] + other[...]
    scale_grad, shift_grad = total[:, :CHANNELS], total[:, CHANNELS:]
    cells, mean, inverse, scale, shift = norm_terms(stats, film)
    grad_film[:, :CHANNELS] = action[...] * scale_grad
    grad_film[:, CHANNELS:] = action[...] * shift_grad
    swap = swap_matrix(None)
    live = (iota((256, 1), 0) & 15) < counts[0]
    for g in range(4):
        part = slice(16 * g, 16 * g + 16)
        x = held[part, :, :].reshape(256, CHANNELS).astype(F32)
        normed = (x - mean) * inverse
        value = kept[256 * g : 256 * g + 256, :] - inverse * (
            scale * shift_grad / cells + normed * scale * scale_grad / cells
        )
        value = jnp.where(live, value, 0.0).astype(BF16)
        grad_inputs[:, part, :] = dot(swap, value).astype(BF16).reshape(16, 16, CHANNELS)


def unpack_kernel(tiles, grad_weight):
    zero = jnp.zeros((16, 128), BF16)
    thirds = [
        jnp.concatenate([tiles[3 * u + n] for u in range(10)] + [last], axis=0)
        for n, last in enumerate((tiles[30], zero, tiles[31]))
    ]
    even = jnp.concatenate([thirds[0], thirds[2][:, :64]], axis=1)
    odd = jnp.concatenate([thirds[1], thirds[2][:, 64:]], axis=1)
    row, col = iota((384, 352), 0), iota((384, 352), 1)
    k = row & 31
    chosen = (k < 27) & (col == (row >> 5) + 12 * (k >> 1) + 176 * (k & 1))
    chosen = jnp.where(chosen, 1.0, 0.0).astype(BF16)
    found = dot(chosen, jnp.concatenate([even, odd], axis=0)).reshape(12, 32, CHANNELS)
    grad_weight[...] = found[:, :27, :]


SMEM = pl.BlockSpec(memory_space=pltpu.SMEM)
VMEM = pl.BlockSpec(memory_space=pltpu.VMEM)
ANY = pl.BlockSpec(memory_space=pl.ANY)


def call(kernel, scalars, arrays, outs, scratch=(), flops=0, name=None, left=0, sems=None):
    sems = left if sems is None else sems
    shapes = [jax.ShapeDtypeStruct(shape, dtype) for shape, dtype in outs]
    moved = sum(x.size * x.dtype.itemsize for x in [*arrays, *shapes])
    return pl.pallas_call(
        kernel,
        out_shape=shapes,
        in_specs=[SMEM] * len(scalars) + [VMEM] * (len(arrays) - left) + [ANY] * left,
        out_specs=[VMEM] * len(outs),
        scratch_shapes=[pltpu.VMEM(*s) for s in scratch]
        + ([pltpu.SemaphoreType.DMA((sems,))] if sems else []),
        compiler_params=pltpu.CompilerParams(vmem_limit_bytes=VMEM_LIMIT),
        cost_estimate=pl.CostEstimate(flops=flops, bytes_accessed=moved, transcendentals=0),
        name=name,
    )(*scalars, *arrays)


def exchange(array, axis, groups=None):
    return lax.all_to_all(array, axis, 0, 0, axis_index_groups=groups, tiled=True)


def body(features, cotangent, counts, neighbours, send_x, send_y, action, conv_weight, film_weight):
    size_x, size_y = lax.axis_size("gx"), lax.axis_size("gy")
    count = counts.reshape(1)
    rule = neighbours[0, 0]
    block = ((VOXELS, 16, CHANNELS), BF16)
    face = ((16, 16, CHANNELS), BF16)
    spaced = ((6, 6, 6, 16, CHANNELS), BF16)
    joined = ((16, 16, 384), BF16)
    held, up, stats, faces, film = call(
        pack_kernel,
        [count, send_x[0, 0]],
        [features[0, 0], cotangent[0, 0], action[None], film_weight],
        [block, block, ((size_x, 4, 128), F32), ((2, *face[0]), BF16), ((1, 2 * CHANNELS), F32)],
        flops=10**9,
        name="pack",
    )
    up_x = [(i, i + 1) for i in range(size_x - 1)]
    down_x = [(i + 1, i) for i in range(size_x - 1)]
    up_y = [(i, i + 1) for i in range(size_y - 1)]
    down_y = [(i + 1, i) for i in range(size_y - 1)]
    lower = lax.ppermute(faces[1], "gx", up_x)
    upper = lax.ppermute(faces[0], "gx", down_x)
    stats = exchange(stats, "gx")
    weight = jnp.transpose(conv_weight, (1, 0, 2))
    face_low, face_high, stats = call(
        cross_kernel,
        [send_y[0, 0]],
        [held, up, lower, upper, stats],
        [joined, joined, ((size_y, 4, 128), F32)],
        flops=10**8,
        name="cross",
    )
    side_l = lax.ppermute(face_high, "gy", up_y)
    side_u = lax.ppermute(face_low, "gy", down_y)
    stats = exchange(stats, "gy")
    core = lax.axis_index("gx") & 1
    swapped = [(i, i ^ 1) for i in range(size_x)]
    fields = [held, up, lower, upper, side_l, side_u, rule, stats, film]
    half = ((8, TILES, 16, 384), BF16)
    near, far, padded = call(
        weight_kernel,
        [count, core.reshape(1)],
        fields,
        [half, half, spaced],
        [block, face, face, face, face, ((4, 256, 1024), BF16)],
        flops=4 * 10**9,
        name="weight",
    )
    other = lax.ppermute(far, "gx", swapped)
    taps = ((27, CHANNELS, CHANNELS), BF16)
    total = ((1024, CHANNELS), F32)
    kept, sums = call(
        back_kernel,
        [count],
        [*fields, weight],
        [total, ((1, 2 * CHANNELS), F32)],
        [spaced, total, face, face, taps],
        flops=3 * 10**9,
        name="back",
        left=1,
    )
    (parts,) = call(combine_kernel, [], [near, other, sums], [half], name="combine")
    parts = exchange(parts, "gx", [list(range(c, size_x, 2)) for c in range(2)])
    (output,) = call(
        forward_kernel,
        [count],
        [held, weight, padded],
        [((SLOTS, VOXELS, CHANNELS), BF16)],
        [total, taps, spaced],
        flops=3 * 10**9,
        name="forward",
        left=2,
    )
    (shares,) = call(
        share_kernel, [], [parts, output], [((size_y, 24, 128), BF16)], name="share", left=1, sems=0
    )
    shares = exchange(shares, "gy")
    mine, sums = call(
        own_kernel, [], [shares], [((size_y, 16, 128), BF16), ((1, 2 * CHANNELS), F32)], name="own"
    )
    other = lax.ppermute(sums, "gx", swapped)
    tiles = exchange(mine, "gy")
    grad_film, grad_inputs = call(
        finish_kernel,
        [count],
        [sums, other, stats, film, action[:, None], held, kept],
        [((128, 2 * CHANNELS), F32), ((SLOTS, VOXELS, CHANNELS), BF16)],
        flops=10**9,
        name="finish",
    )
    (grad_weight,) = call(unpack_kernel, [], [tiles], [((12, 27, CHANNELS), F32)], name="unpack")
    return output[None, None], grad_inputs[None, None], grad_weight, grad_film


def solution(mesh):
    tile = P("gx", "gy")
    return jax.shard_map(
        body,
        mesh=mesh,
        in_specs=(tile, tile, tile, tile, tile, tile, P(), P(), P()),
        out_specs=(tile, tile, P("gx"), P()),
        check_vma=False,
    )
```

```python
import jax
import jax.numpy as jnp
from jax import lax
from jax.experimental import pallas as pl
from jax.experimental.pallas import tpu as pltpu
from jax.sharding import PartitionSpec as P

SLOTS = 16
VOXELS = 64
CHANNELS = 192
TILES = 11
MIB = 1024 * 1024
F32 = jnp.float32
BF16 = jnp.bfloat16


def iota(shape, dim):
    return lax.broadcasted_iota(jnp.int32, shape, dim)


def dot(left, right):
    return jnp.dot(left, right, preferred_element_type=F32)


def dot_nt(left, right):
    return lax.dot_general(left, right, (((1,), (1,)), ((), ())), preferred_element_type=F32)


def swap_matrix(count):
    row, col = iota((256, 256), 0), iota((256, 256), 1)
    hit = ((row >> 4) == (col & 15)) & ((row & 15) == (col >> 4))
    if count is not None:
        hit = hit & ((row & 15) < count)
    return jnp.where(hit, 1.0, 0.0).astype(BF16)


def list_column(ref, side, length, rows, half):
    row = iota((rows, 1), 0)
    entry = jnp.full((rows, 1), -1, jnp.int32)
    for e in range(length):
        value = ref[side, e]
        entry = jnp.where((row == e) | (row == e + half), value, entry)
    return entry


def pick(column, width, low, high, base, second, half):
    rows = column.shape[0]
    row, col = iota((rows, width), 0), iota((rows, width), 1)
    target = column - low + base + jnp.where(row >= half, second, 0)
    hit = (column >= low) & (column < high) & (col == target)
    return jnp.where(hit, 1.0, 0.0).astype(BF16)


def pack_lines(first, second):
    rest = jnp.concatenate([first[:, 128:], second[:, 128:]], axis=1)
    return [first[:, :128], second[:, :128], rest]


def unpack_lines(lines):
    first = jnp.concatenate([lines[0:1], lines[2:3, :64]], axis=1)
    second = jnp.concatenate([lines[1:2], lines[2:3, 64:]], axis=1)
    return first, second


def stack_lines(lines, rows):
    row = iota((rows, 128), 0)
    block = jnp.zeros((rows, 128), F32)
    for e, line in enumerate(lines):
        block = jnp.where(row == e, line, block)
    return block


def join_fields(value):
    first, second = value[0:16], value[16:32]
    rest = jnp.concatenate([first[:, 128:], second[:, 128:]], axis=1)
    return jnp.concatenate([first[:, :128], second[:, :128], rest], axis=1).astype(BF16)


def one_field(joined, which):
    tail = joined[..., 256:320] if which == 0 else joined[..., 320:384]
    return jnp.concatenate([joined[..., 128 * which : 128 * which + 128], tail], axis=-1)


def pack_kernel(
    counts, send_x, feat, cot, action, film_weight, held, up, stats, face_low, face_high, film
):
    swap = swap_matrix(counts[0])
    total = jnp.zeros((1, CHANNELS), F32)
    square = jnp.zeros((1, CHANNELS), F32)
    for g in range(4):
        part = slice(16 * g, 16 * g + 16)
        moved = dot(swap, feat[:, part, :].reshape(256, CHANNELS))
        total += jnp.sum(moved, axis=0, keepdims=True)
        square += jnp.sum(moved * moved, axis=0, keepdims=True)
        held[part, :, :] = moved.astype(BF16).reshape(16, 16, CHANNELS)
        moved = dot(swap, cot[:, part, :].reshape(256, CHANNELS))
        up[part, :, :] = moved.astype(BF16).reshape(16, 16, CHANNELS)
    cells = (counts[0] * VOXELS).astype(F32)
    block = stack_lines(pack_lines(total, square) + [cells], 4)
    for i in range(stats.shape[0]):
        stats[i, :, :] = block
    for side in range(2):
        chosen = pick(list_column(send_x, side, 8, 16, 8), 32, 0, SLOTS, 0, 16, 8)
        for i in range(16):
            both = jnp.concatenate([held[48 * side + i], up[48 * side + i]], axis=0)
            target = (face_low, face_high)[side]
            target[i, :, :] = dot(chosen, both).astype(BF16)
    film[...] = lax.dot_general(
        action[...],
        film_weight[...],
        (((1,), (0,)), ((), ())),
        precision=lax.Precision.HIGHEST,
        preferred_element_type=F32,
    )


def cross_kernel(send_y, held, up, lower, upper, stats, face_low, face_high, spread):
    block = jnp.sum(stats[...], axis=0)
    for i in range(spread.shape[0]):
        spread[i, :, :] = block
    for side in range(2):
        target = (face_low, face_high)[side]
        column = list_column(send_y, side, 12, 32, 16)
        local = pick(column, 32, 0, SLOTS, 0, 16, 16)
        from_lower = pick(column, 16, 17, 25, 0, 8, 16)
        from_upper = pick(column, 16, 25, 33, 0, 8, 16)
        for a in range(4):
            for c in range(4):
                v = 16 * a + 12 * side + c
                value = dot(local, jnp.concatenate([held[v], up[v]], axis=0))
                if a == 3:
                    value += dot(from_lower, lower[12 * side + c])
                if a == 0:
                    value += dot(from_upper, upper[12 * side + c])
                target[4 * a + c, :, :] = join_fields(value)


def norm_terms(stats, film):
    lines = jnp.sum(stats[...], axis=0)
    total, square = unpack_lines(lines)
    cells = lines[3:4, 0:1]
    mean = total / cells
    variance = square / cells - mean * mean
    inverse = lax.rsqrt(variance + 1e-05)
    scale = 1.0 + film[:, :CHANNELS]
    shift = film[:, CHANNELS:]
    return cells, mean, inverse, scale, shift


def gather_blocks(rule, half, own, low, high, low_y, high_y, padded):
    entries = rule[...]
    col = iota((16, 80), 1)
    hot = []
    for n in range(27):
        column = entries[:, n : n + 1]
        target = jnp.where(column >= 17, column - 1 + half, column)
        target = jnp.where(column >= 25, column + 7 + half, target)
        target = jnp.where(column >= 33, column + 15, target)
        target = jnp.where(column >= 45, column + 19, target)
        hit = (column != 16) & (col == target)
        hot.append(jnp.where(hit, 1.0, 0.0).astype(BF16))
    none = jnp.zeros((16, CHANNELS), BF16)
    for a in range(4):
        for b in range(4):
            for c in range(4):
                mine = own[16 * a + 4 * b + c]
                padded[a + 1, b + 1, c + 1, :, :] = mine
                ways = [
                    [(q + 1, 0)] + ([(5, 1)] if q == 0 else []) + ([(0, -1)] if q == 3 else [])
                    for q in (a, b, c)
                ]
                places = [(x, y, z) for x in ways[0] for y in ways[1] for z in ways[2]][1:]
                if not places:
                    continue
                listed = jnp.concatenate(
                    [
                        mine,
                        low[4 * b + c] if a == 3 else none,
                        high[4 * b + c] if a == 0 else none,
                        low_y[4 * a + c] if b == 3 else none,
                        high_y[4 * a + c] if b == 0 else none,
                    ],
                    axis=0,
                )
                chosen = jnp.concatenate(
                    [hot[9 * (x[1] + 1) + 3 * (y[1] + 1) + z[1] + 1] for x, y, z in places], axis=0
                )
                found = dot(chosen, listed).astype(BF16)
                for m, (x, y, z) in enumerate(places):
                    padded[x[0], y[0], z[0], :, :] = found[16 * m : 16 * m + 16]


def window(padded, k):
    x, y, z = k // 9, (k // 3) % 3, k % 3
    part = padded[pl.ds(x, 4), pl.ds(y, 4), pl.ds(z, 4), :, :]
    return part.reshape(1024, CHANNELS)


def early_kernel(
    held, up, lower, upper, side_l, side_u, rule, weight_at,
    raw, back, turned, wide, low_y, high_y, weight, done,
):
    copy = pltpu.make_async_copy(weight_at, weight, done.at[0])
    copy.start()
    for which, own, target in ((0, held, raw), (1, up, wide)):
        low_y[...] = one_field(side_l[...], which)
        high_y[...] = one_field(side_u[...], which)
        gather_blocks(rule, 8 * which, own, lower, upper, low_y, high_y, target)
    same = jnp.where(iota((CHANNELS, CHANNELS), 0) == iota((CHANNELS, CHANNELS), 1), 1.0, 0.0)
    turned[...] = dot_nt(same.astype(BF16), up[...].reshape(1024, CHANNELS)).astype(BF16)
    back[...] = jnp.zeros_like(back)
    copy.wait()

    def step(t, carry):
        k = 3 * t
        total = dot(window(wide, k), weight[26 - k])
        total += dot(window(wide, k + 1), weight[25 - k])
        back[...] += total + dot(window(wide, k + 2), weight[24 - k])
        return carry

    lax.fori_loop(0, 9, step, 0)


def weight_kernel(
    counts, core, raw, up_turned, rule, stats, film,
    near, far, padded, turned,
):
    cells, mean, inverse, scale, shift = norm_terms(stats, film)
    live = iota((16, 1), 0) < counts[0]
    entries = rule[...]

    def act(at, mask):
        x = raw[at]
        lead = x.shape[:-2]
        x = (x.astype(F32).reshape(-1, CHANNELS) - mean) * inverse * scale + shift
        x = jnp.maximum(x, 0.0).reshape(-1, 16, CHANNELS)
        x = jnp.where(mask[None], x, 0.0).astype(BF16)
        padded[at] = x.reshape(*lead, 16, CHANNELS)

    ranges = (slice(0, 1), slice(1, 5), slice(5, 6))
    for n in range(27):
        x, y, z = n // 9, n // 3 % 3, n % 3
        if n == 13:
            for a in range(1, 5):
                act((slice(a, a + 1), ranges[1], ranges[1]), live)
        else:
            act((ranges[x], ranges[y], ranges[z]), entries[:, n : n + 1] != 16)

    row, col = iota((256, CHANNELS), 0), iota((256, CHANNELS), 1)
    group = ((row >> 4) & 7) * 2 + jnp.where(row >= 128, 1 - core[0], core[0])
    for m in range(4):
        place = (row + 4 * m) & 15
        spread = (place < 12) & (col == group * 12 + place)
        spread = jnp.where(spread, 1.0, 0.0).astype(BF16)
        turned[m, :, :] = dot(spread, up_turned[...]).astype(BF16)

    line = iota((256, 384), 0) & 15

    def pair(m, k1, k2):
        grad1 = dot(turned[m], window(padded, k1))
        grad2 = dot(turned[m], window(padded, k2)) if k2 is not None else jnp.zeros_like(grad1)
        rest = jnp.concatenate([grad1[:, 128:], grad2[:, 128:]], axis=1)
        return jnp.concatenate([grad1[:, :128], grad2[:, :128], rest], axis=1)

    def store(at, value):
        value = value.astype(BF16).reshape(16, 1, 16, 384)
        near[:, pl.ds(at, 1), :, :] = value[:8]
        far[:, pl.ds(at, 1), :, :] = value[8:]

    def step(q, carry):
        k = 8 * q
        first, second = pair(0, k, k + 1), pair(1, k + 2, k + 3)
        store(3 * q, jnp.where(line < 12, first, second))
        third = pair(2, k + 4, k + 5)
        store(3 * q + 1, jnp.where(line < 8, second, third))
        fourth = pair(3, k + 6, k + 7)
        store(3 * q + 2, jnp.where(line < 4, third, fourth))
        return carry

    lax.fori_loop(0, 3, step, 0)
    first, second = pair(0, 24, 25), pair(1, 26, None)
    store(9, jnp.where(line < 12, first, second))
    store(10, jnp.where(line < 8, second, 0.0))


def split(value):
    first = value.astype(BF16).astype(F32)
    second = (value - first).astype(BF16).astype(F32)
    return first, second, value - first - second


def slope_kernel(counts, held, up, back, stats, film, kept, lines):
    cells, mean, inverse, scale, shift = norm_terms(stats, film)
    shift_grad = jnp.zeros((1, CHANNELS), F32)
    scale_grad = jnp.zeros((1, CHANNELS), F32)
    live = (iota((256, 1), 0) & 15) < counts[0]
    for g in range(4):
        at = slice(256 * g, 256 * g + 256)
        part = slice(16 * g, 16 * g + 16)
        x = held[part, :, :].reshape(256, CHANNELS).astype(F32)
        normed = (x - mean) * inverse
        slope = jnp.where(live & (normed * scale + shift > 0), back[at, :], 0.0)
        shift_grad += jnp.sum(slope, axis=0, keepdims=True)
        scale_grad += jnp.sum(slope * normed, axis=0, keepdims=True)
        kept[at, :] = up[part, :, :].reshape(256, CHANNELS).astype(F32) + inverse * (slope * scale)
    row = iota((16, 384), 0)
    block = jnp.zeros((16, 384), F32)
    for e, piece in enumerate(split(jnp.concatenate([scale_grad, shift_grad], axis=1))):
        block = jnp.where(row == 8 + e, piece, block)
    lines[...] = block


def forward_kernel(counts, held, weight_at, padded_at, output, token, acc, weight, padded, done):
    token[...] = jnp.zeros_like(token)
    copies = [
        pltpu.make_async_copy(weight_at, weight, done.at[0]),
        pltpu.make_async_copy(padded_at, padded, done.at[1]),
    ]
    for copy in copies:
        copy.start()
    acc[...] = jnp.zeros_like(acc)
    for copy in copies:
        copy.wait()

    def step(t, carry):
        k = 3 * t
        total = dot_nt(window(padded, k), weight[k])
        total += dot_nt(window(padded, k + 1), weight[k + 1])
        acc[...] += total + dot_nt(window(padded, k + 2), weight[k + 2])
        return carry

    lax.fori_loop(0, 9, step, 0)
    swap = swap_matrix(None)
    live = (iota((256, 1), 0) & 15) < counts[0]
    for g in range(4):
        part = slice(16 * g, 16 * g + 16)
        x = held[part, :, :].reshape(256, CHANNELS).astype(F32)
        mixed = jnp.where(live, x + acc[256 * g : 256 * g + 256, :], 0.0).astype(BF16)
        output[:, part, :] = dot(swap, mixed).astype(BF16).reshape(16, 16, CHANNELS)


def place_of(share):
    return (share // 3, share % 3) if share < 30 else (10, 2 * (share - 30))


def share_kernel(parts, token, shares):
    for tile in reversed(range(TILES)):
        total = jnp.sum(parts[:, tile, :, :].astype(F32), axis=0)
        if tile == TILES - 1:
            sums = total[8:9] + total[9:10] + total[10:11]
            pieces = split(sums)[:2]
            lines = [piece[:, 128 * m : 128 * m + 128] for piece in pieces for m in range(3)]
            block = stack_lines(lines, 8)
        for share in range(32):
            if place_of(share)[0] == tile:
                third = place_of(share)[1]
                mine = total[:, 128 * third : 128 * third + 128]
                shares[share, :, :] = jnp.concatenate([mine, block], axis=0).astype(BF16)


def own_kernel(parts, mine, sums):
    total = jnp.sum(parts[...].astype(F32), axis=0)
    for i in range(mine.shape[0]):
        mine[i, :, :] = total[0:16].astype(BF16)
    lines = total[16:19] + total[19:22]
    sums[...] = jnp.concatenate([lines[0:1], lines[1:2], lines[2:3]], axis=1)


def finish_kernel(counts, sums, other, stats, film, action, held, kept, grad_film, grad_inputs):
    total = sums[...] + other[...]
    scale_grad, shift_grad = total[:, :CHANNELS], total[:, CHANNELS:]
    cells, mean, inverse, scale, shift = norm_terms(stats, film)
    grad_film[:, :CHANNELS] = action[...] * scale_grad
    grad_film[:, CHANNELS:] = action[...] * shift_grad
    swap = swap_matrix(None)
    live = (iota((256, 1), 0) & 15) < counts[0]
    for g in range(4):
        part = slice(16 * g, 16 * g + 16)
        x = held[part, :, :].reshape(256, CHANNELS).astype(F32)
        normed = (x - mean) * inverse
        value = kept[256 * g : 256 * g + 256, :] - inverse * (
            scale * shift_grad / cells + normed * scale * scale_grad / cells
        )
        value = jnp.where(live, value, 0.0).astype(BF16)
        grad_inputs[:, part, :] = dot(swap, value).astype(BF16).reshape(16, 16, CHANNELS)


def unpack_kernel(tiles, grad_weight):
    zero = jnp.zeros((16, 128), BF16)
    thirds = [
        jnp.concatenate([tiles[3 * u + n] for u in range(10)] + [last], axis=0)
        for n, last in enumerate((tiles[30], zero, tiles[31]))
    ]
    even = jnp.concatenate([thirds[0], thirds[2][:, :64]], axis=1)
    odd = jnp.concatenate([thirds[1], thirds[2][:, 64:]], axis=1)
    row, col = iota((384, 352), 0), iota((384, 352), 1)
    k = row & 31
    chosen = (k < 27) & (col == (row >> 5) + 12 * (k >> 1) + 176 * (k & 1))
    chosen = jnp.where(chosen, 1.0, 0.0).astype(BF16)
    found = dot(chosen, jnp.concatenate([even, odd], axis=0)).reshape(12, 32, CHANNELS)
    grad_weight[...] = found[:, :27, :]


SMEM = pl.BlockSpec(memory_space=pltpu.SMEM)
VMEM = pl.BlockSpec(memory_space=pltpu.VMEM)
ANY = pl.BlockSpec(memory_space=pl.ANY)


def call(kernel, scalars, arrays, outs, scratch=(), flops=0, name=None, left=0, room=12):
    shapes = [jax.ShapeDtypeStruct(shape, dtype) for shape, dtype in outs]
    moved = sum(x.size * x.dtype.itemsize for x in [*arrays, *shapes])
    return pl.pallas_call(
        kernel,
        out_shape=shapes,
        in_specs=[SMEM] * len(scalars) + [VMEM] * (len(arrays) - left) + [ANY] * left,
        out_specs=[VMEM] * len(outs),
        scratch_shapes=[pltpu.VMEM(*s) for s in scratch]
        + ([pltpu.SemaphoreType.DMA((left,))] if left else []),
        compiler_params=pltpu.CompilerParams(vmem_limit_bytes=room * MIB),
        cost_estimate=pl.CostEstimate(flops=flops, bytes_accessed=moved, transcendentals=0),
        name=name,
    )(*scalars, *arrays)


def exchange(array, axis, groups=None):
    return lax.all_to_all(array, axis, 0, 0, axis_index_groups=groups, tiled=True)


def body(features, cotangent, counts, neighbours, send_x, send_y, action, conv_weight, film_weight):
    size_x, size_y = lax.axis_size("gx"), lax.axis_size("gy")
    count = counts.reshape(1)
    rule = neighbours[0, 0]
    block = ((VOXELS, 16, CHANNELS), BF16)
    face = ((16, 16, CHANNELS), BF16)
    spaced = ((6, 6, 6, 16, CHANNELS), BF16)
    joined = ((16, 16, 384), BF16)
    held, up, stats, face_low, face_high, film = call(
        pack_kernel,
        [count, send_x[0, 0]],
        [features[0, 0], cotangent[0, 0], action[None], film_weight],
        [block, block, ((size_x, 4, 128), F32), face, face, ((1, 2 * CHANNELS), F32)],
        flops=10**9,
        name="pack",
    )
    up_x = [(i, i + 1) for i in range(size_x - 1)]
    down_x = [(i + 1, i) for i in range(size_x - 1)]
    up_y = [(i, i + 1) for i in range(size_y - 1)]
    down_y = [(i + 1, i) for i in range(size_y - 1)]
    lower = lax.ppermute(face_high, "gx", up_x)
    upper = lax.ppermute(face_low, "gx", down_x)
    stats = exchange(stats, "gx")
    weight = jnp.transpose(conv_weight, (1, 0, 2))
    face_low, face_high, stats = call(
        cross_kernel,
        [send_y[0, 0]],
        [held, up, lower, upper, stats],
        [joined, joined, ((size_y, 4, 128), F32)],
        flops=10**8,
        name="cross",
    )
    side_l = lax.ppermute(face_high, "gy", up_y)
    side_u = lax.ppermute(face_low, "gy", down_y)
    stats = exchange(stats, "gy")
    core = lax.axis_index("gx") & 1
    swapped = [(i, i ^ 1) for i in range(size_x)]
    taps = ((27, CHANNELS, CHANNELS), BF16)
    total = ((1024, CHANNELS), F32)
    raw, back, turned = call(
        early_kernel,
        [],
        [held, up, lower, upper, side_l, side_u, rule, weight],
        [spaced, total, ((CHANNELS, 1024), BF16)],
        [spaced, face, face, taps],
        flops=3 * 10**9,
        name="early",
        left=1,
        room=20,
    )
    half = ((8, TILES, 16, 384), BF16)
    near, far, padded = call(
        weight_kernel,
        [count, core.reshape(1)],
        [raw, turned, rule, stats, film],
        [half, half, spaced],
        [((4, 256, 1024), BF16)],
        flops=4 * 10**9,
        name="weight",
        room=20,
    )
    other = lax.ppermute(far, "gx", swapped)
    kept, lines = call(
        slope_kernel,
        [count],
        [held, up, back, stats, film],
        [total, ((16, 384), F32)],
        flops=10**8,
        name="slope",
    )
    tile = lax.broadcasted_iota(jnp.int32, half[0], 1)
    row = lax.broadcasted_iota(jnp.int32, half[0], 2)
    parts = near.astype(F32) + other.astype(F32)
    parts = jnp.where((tile == TILES - 1) & (row >= 8), lines, parts).astype(BF16)
    parts = exchange(parts, "gx", [list(range(c, size_x, 2)) for c in range(2)])
    output, token = call(
        forward_kernel,
        [count],
        [held, weight, padded],
        [((SLOTS, VOXELS, CHANNELS), BF16), ((8, 128), F32)],
        [total, taps, spaced],
        flops=3 * 10**9,
        name="forward",
        left=2,
        room=16,
    )
    (shares,) = call(share_kernel, [], [parts, token], [((size_y, 24, 128), BF16)], name="share")
    shares = exchange(shares, "gy")
    mine, sums = call(
        own_kernel, [], [shares], [((size_y, 16, 128), BF16), ((1, 2 * CHANNELS), F32)], name="own"
    )
    other = lax.ppermute(sums, "gx", swapped)
    tiles = exchange(mine, "gy")
    grad_film, grad_inputs = call(
        finish_kernel,
        [count],
        [sums, other, stats, film, action[:, None], held, kept],
        [((128, 2 * CHANNELS), F32), ((SLOTS, VOXELS, CHANNELS), BF16)],
        flops=10**9,
        name="finish",
    )
    (grad_weight,) = call(unpack_kernel, [], [tiles], [((12, 27, CHANNELS), F32)], name="unpack")
    return output[None, None], grad_inputs[None, None], grad_weight, grad_film


def solution(mesh):
    tile = P("gx", "gy")
    return jax.shard_map(
        body,
        mesh=mesh,
        in_specs=(tile, tile, tile, tile, tile, tile, P(), P(), P()),
        out_specs=(tile, tile, P("gx"), P()),
        check_vma=False,
    )
```

```python
import math

import jax
import jax.numpy as jnp
from jax import lax
from jax.experimental import pallas as pl
from jax.experimental.pallas import tpu as pltpu
from jax.sharding import PartitionSpec as P

SLOTS = 16
VOXELS = 64
CHANNELS = 192
TILES = 11
MIB = 1024 * 1024
F32 = jnp.float32
BF16 = jnp.bfloat16


def iota(shape, dim):
    return lax.broadcasted_iota(jnp.int32, shape, dim)


def dot(left, right):
    return jnp.dot(left, right, preferred_element_type=F32)


def dot_nt(left, right):
    return lax.dot_general(left, right, (((1,), (1,)), ((), ())), preferred_element_type=F32)


def swap_matrix(count):
    row, col = iota((256, 256), 0), iota((256, 256), 1)
    hit = ((row >> 4) == (col & 15)) & ((row & 15) == (col >> 4))
    if count is not None:
        hit = hit & ((row & 15) < count)
    return jnp.where(hit, 1.0, 0.0).astype(BF16)


def list_column(ref, side, length, rows, half):
    row = iota((rows, 1), 0)
    entry = jnp.full((rows, 1), -1, jnp.int32)
    for e in range(length):
        value = ref[side, e]
        entry = jnp.where((row == e) | (row == e + half), value, entry)
    return entry


def pick(column, width, low, high, base, second, half):
    rows = column.shape[0]
    row, col = iota((rows, width), 0), iota((rows, width), 1)
    target = column - low + base + jnp.where(row >= half, second, 0)
    hit = (column >= low) & (column < high) & (col == target)
    return jnp.where(hit, 1.0, 0.0).astype(BF16)


def pack_lines(first, second):
    rest = jnp.concatenate([first[:, 128:], second[:, 128:]], axis=1)
    return [first[:, :128], second[:, :128], rest]


def unpack_lines(lines):
    first = jnp.concatenate([lines[0:1], lines[2:3, :64]], axis=1)
    second = jnp.concatenate([lines[1:2], lines[2:3, 64:]], axis=1)
    return first, second


def stack_lines(lines, rows):
    row = iota((rows, 128), 0)
    block = jnp.zeros((rows, 128), F32)
    for e, line in enumerate(lines):
        block = jnp.where(row == e, line, block)
    return block


def join_fields(value):
    first, second = value[0:16], value[16:32]
    rest = jnp.concatenate([first[:, 128:], second[:, 128:]], axis=1)
    return jnp.concatenate([first[:, :128], second[:, :128], rest], axis=1).astype(BF16)


def one_field(joined, which):
    tail = joined[..., 256:320] if which == 0 else joined[..., 320:384]
    return jnp.concatenate([joined[..., 128 * which : 128 * which + 128], tail], axis=-1)


def pack_kernel(
    counts, send_x, feat_at, cot_at, film_at, action_at,
    held, up, stats, face_low, face_high, film, feat, cot, film_weight, action, done,
):
    pairs = ((feat_at, feat), (cot_at, cot), (film_at, film_weight), (action_at, action))
    copies = [
        pltpu.make_async_copy(source, target, done.at[n]) for n, (source, target) in enumerate(pairs)
    ]
    for copy in copies:
        copy.start()
    swap = swap_matrix(counts[0])
    for copy in copies:
        copy.wait()
    total = jnp.zeros((1, CHANNELS), F32)
    square = jnp.zeros((1, CHANNELS), F32)
    for g in range(4):
        part = slice(16 * g, 16 * g + 16)
        moved = dot(swap, feat[:, part, :].reshape(256, CHANNELS))
        total += jnp.sum(moved, axis=0, keepdims=True)
        square += jnp.sum(moved * moved, axis=0, keepdims=True)
        held[part, :, :] = moved.astype(BF16).reshape(16, 16, CHANNELS)
        moved = dot(swap, cot[:, part, :].reshape(256, CHANNELS))
        up[part, :, :] = moved.astype(BF16).reshape(16, 16, CHANNELS)
    cells = (counts[0] * VOXELS).astype(F32)
    block = stack_lines(pack_lines(total, square) + [cells], 4)
    for i in range(stats.shape[0]):
        stats[i, :, :] = block
    for side in range(2):
        chosen = pick(list_column(send_x, side, 8, 16, 8), 32, 0, SLOTS, 0, 16, 8)
        for i in range(16):
            both = jnp.concatenate([held[48 * side + i], up[48 * side + i]], axis=0)
            target = (face_low, face_high)[side]
            target[i, :, :] = dot(chosen, both).astype(BF16)
    film[...] = lax.dot_general(
        action[...],
        film_weight[...],
        (((1,), (0,)), ((), ())),
        precision=lax.Precision.HIGHEST,
        preferred_element_type=F32,
    )


def cross_kernel(send_y, held, up, lower, upper, stats, face_low, face_high, spread):
    block = jnp.sum(stats[...], axis=0)
    for i in range(spread.shape[0]):
        spread[i, :, :] = block
    for side in range(2):
        target = (face_low, face_high)[side]
        column = list_column(send_y, side, 12, 32, 16)
        local = pick(column, 32, 0, SLOTS, 0, 16, 16)
        from_lower = pick(column, 16, 17, 25, 0, 8, 16)
        from_upper = pick(column, 16, 25, 33, 0, 8, 16)
        for a in range(4):
            for c in range(4):
                v = 16 * a + 12 * side + c
                value = dot(local, jnp.concatenate([held[v], up[v]], axis=0))
                if a == 3:
                    value += dot(from_lower, lower[12 * side + c])
                if a == 0:
                    value += dot(from_upper, upper[12 * side + c])
                target[4 * a + c, :, :] = join_fields(value)


def norm_terms(stats, film):
    lines = jnp.sum(stats[...], axis=0)
    total, square = unpack_lines(lines)
    cells = lines[3:4, 0:1]
    mean = total / cells
    variance = square / cells - mean * mean
    inverse = lax.rsqrt(variance + 1e-05)
    scale = 1.0 + film[:, :CHANNELS]
    shift = film[:, CHANNELS:]
    return cells, mean, inverse, scale, shift


def gather_blocks(rule, half, own, low, high, low_y, high_y, padded):
    entries = rule[...]
    col = iota((16, 80), 1)
    hot = []
    for n in range(27):
        column = entries[:, n : n + 1]
        target = jnp.where(column >= 17, column - 1 + half, column)
        target = jnp.where(column >= 25, column + 7 + half, target)
        target = jnp.where(column >= 33, column + 15, target)
        target = jnp.where(column >= 45, column + 19, target)
        hit = (column != 16) & (col == target)
        hot.append(jnp.where(hit, 1.0, 0.0).astype(BF16))
    none = jnp.zeros((16, CHANNELS), BF16)
    for a in range(4):
        for b in range(4):
            for c in range(4):
                mine = own[16 * a + 4 * b + c]
                padded[a + 1, b + 1, c + 1, :, :] = mine
                ways = [
                    [(q + 1, 0)] + ([(5, 1)] if q == 0 else []) + ([(0, -1)] if q == 3 else [])
                    for q in (a, b, c)
                ]
                places = [(x, y, z) for x in ways[0] for y in ways[1] for z in ways[2]][1:]
                if not places:
                    continue
                listed = jnp.concatenate(
                    [
                        mine,
                        low[4 * b + c] if a == 3 else none,
                        high[4 * b + c] if a == 0 else none,
                        low_y[4 * a + c] if b == 3 else none,
                        high_y[4 * a + c] if b == 0 else none,
                    ],
                    axis=0,
                )
                chosen = jnp.concatenate(
                    [hot[9 * (x[1] + 1) + 3 * (y[1] + 1) + z[1] + 1] for x, y, z in places], axis=0
                )
                found = dot(chosen, listed).astype(BF16)
                for m, (x, y, z) in enumerate(places):
                    padded[x[0], y[0], z[0], :, :] = found[16 * m : 16 * m + 16]


def window(padded, k):
    x, y, z = k // 9, (k // 3) % 3, k % 3
    part = padded[pl.ds(x, 4), pl.ds(y, 4), pl.ds(z, 4), :, :]
    return part.reshape(1024, CHANNELS)


def early_kernel(
    held, up, lower, upper, side_l, side_u, rule, weight_at,
    raw_at, back, turned, raw, wide, low_y, high_y, weight, done,
):
    copy = pltpu.make_async_copy(weight_at, weight, done.at[0])
    copy.start()
    for which, own, target in ((0, held, raw), (1, up, wide)):
        low_y[...] = one_field(side_l[...], which)
        high_y[...] = one_field(side_u[...], which)
        gather_blocks(rule, 8 * which, own, lower, upper, low_y, high_y, target)
        if which == 0:
            out = pltpu.make_async_copy(raw, raw_at, done.at[1])
            out.start()
    same = jnp.where(iota((CHANNELS, CHANNELS), 0) == iota((CHANNELS, CHANNELS), 1), 1.0, 0.0)
    turned[...] = dot_nt(same.astype(BF16), up[...].reshape(1024, CHANNELS)).astype(BF16)
    back[...] = jnp.zeros_like(back)
    copy.wait()

    def step(t, carry):
        k = 3 * t
        total = dot(window(wide, k), weight[26 - k])
        total += dot(window(wide, k + 1), weight[25 - k])
        back[...] += total + dot(window(wide, k + 2), weight[24 - k])
        return carry

    lax.fori_loop(0, 9, step, 0)
    out.wait()


def weight_kernel(
    counts, core, up_turned, rule, stats, film, raw_at,
    near, far, padded_at, raw, padded, turned, done,
):
    copy = pltpu.make_async_copy(raw_at, raw, done.at[0])
    copy.start()
    cells, mean, inverse, scale, shift = norm_terms(stats, film)
    row, col = iota((256, CHANNELS), 0), iota((256, CHANNELS), 1)
    group = ((row >> 4) & 7) * 2 + jnp.where(row >= 128, 1 - core[0], core[0])
    for m in range(4):
        place = (row + 4 * m) & 15
        spread = (place < 12) & (col == group * 12 + place)
        spread = jnp.where(spread, 1.0, 0.0).astype(BF16)
        turned[m, :, :] = dot(spread, up_turned[...]).astype(BF16)

    live = iota((16, 1), 0) < counts[0]
    entries = rule[...]

    def act(at, mask):
        x = raw[at]
        lead = x.shape[:-2]
        x = (x.astype(F32).reshape(-1, CHANNELS) - mean) * inverse * scale + shift
        x = jnp.maximum(x, 0.0).reshape(-1, 16, CHANNELS)
        x = jnp.where(mask[None], x, 0.0).astype(BF16)
        padded[at] = x.reshape(*lead, 16, CHANNELS)

    copy.wait()
    ranges = (slice(0, 1), slice(1, 5), slice(5, 6))
    for n in range(27):
        x, y, z = n // 9, n // 3 % 3, n % 3
        if n == 13:
            for a in range(1, 5):
                act((slice(a, a + 1), ranges[1], ranges[1]), live)
        else:
            act((ranges[x], ranges[y], ranges[z]), entries[:, n : n + 1] != 16)

    out = pltpu.make_async_copy(padded, padded_at, done.at[1])
    out.start()
    line = iota((256, 384), 0) & 15

    def pair(m, k1, k2):
        grad1 = dot(turned[m], window(padded, k1))
        grad2 = dot(turned[m], window(padded, k2)) if k2 is not None else jnp.zeros_like(grad1)
        rest = jnp.concatenate([grad1[:, 128:], grad2[:, 128:]], axis=1)
        return jnp.concatenate([grad1[:, :128], grad2[:, :128], rest], axis=1)

    def store(at, value):
        value = value.astype(BF16).reshape(16, 1, 16, 384)
        near[:, pl.ds(at, 1), :, :] = value[:8]
        far[:, pl.ds(at, 1), :, :] = value[8:]

    def step(q, carry):
        k = 8 * q
        first, second = pair(0, k, k + 1), pair(1, k + 2, k + 3)
        store(3 * q, jnp.where(line < 12, first, second))
        third = pair(2, k + 4, k + 5)
        store(3 * q + 1, jnp.where(line < 8, second, third))
        fourth = pair(3, k + 6, k + 7)
        store(3 * q + 2, jnp.where(line < 4, third, fourth))
        return carry

    lax.fori_loop(0, 3, step, 0)
    first, second = pair(0, 24, 25), pair(1, 26, None)
    store(9, jnp.where(line < 12, first, second))
    store(10, jnp.where(line < 8, second, 0.0))
    out.wait()


def split(value):
    first = value.astype(BF16).astype(F32)
    second = (value - first).astype(BF16).astype(F32)
    return first, second, value - first - second


def slope_kernel(counts, held, up, back, stats, film, kept_at, lines, kept, done):
    cells, mean, inverse, scale, shift = norm_terms(stats, film)
    shift_grad = jnp.zeros((1, CHANNELS), F32)
    scale_grad = jnp.zeros((1, CHANNELS), F32)
    live = (iota((256, 1), 0) & 15) < counts[0]
    for g in range(4):
        at = slice(256 * g, 256 * g + 256)
        part = slice(16 * g, 16 * g + 16)
        x = held[part, :, :].reshape(256, CHANNELS).astype(F32)
        normed = (x - mean) * inverse
        slope = jnp.where(live & (normed * scale + shift > 0), back[at, :], 0.0)
        shift_grad += jnp.sum(slope, axis=0, keepdims=True)
        scale_grad += jnp.sum(slope * normed, axis=0, keepdims=True)
        kept[at, :] = up[part, :, :].reshape(256, CHANNELS).astype(F32) + inverse * (slope * scale)
    out = pltpu.make_async_copy(kept, kept_at, done.at[0])
    out.start()
    row = iota((16, 384), 0)
    block = jnp.zeros((16, 384), F32)
    for e, piece in enumerate(split(jnp.concatenate([scale_grad, shift_grad], axis=1))):
        block = jnp.where(row == 8 + e, piece, block)
    lines[...] = block
    out.wait()


def forward_kernel(
    counts, held, weight_at, padded_at, output, token, acc, weight, padded, done,
):
    token[...] = jnp.zeros_like(token)
    copies = [
        pltpu.make_async_copy(weight_at, weight, done.at[0]),
        pltpu.make_async_copy(padded_at, padded, done.at[1]),
    ]
    for copy in copies:
        copy.start()
    acc[...] = jnp.zeros_like(acc)
    for copy in copies:
        copy.wait()

    def step(t, carry):
        k = 3 * t
        total = dot_nt(window(padded, k), weight[k])
        total += dot_nt(window(padded, k + 1), weight[k + 1])
        acc[...] += total + dot_nt(window(padded, k + 2), weight[k + 2])
        return carry

    lax.fori_loop(0, 9, step, 0)
    swap = swap_matrix(None)
    live = (iota((256, 1), 0) & 15) < counts[0]
    for g in range(4):
        part = slice(16 * g, 16 * g + 16)
        x = held[part, :, :].reshape(256, CHANNELS).astype(F32)
        mixed = jnp.where(live, x + acc[256 * g : 256 * g + 256, :], 0.0).astype(BF16)
        output[:, part, :] = dot(swap, mixed).astype(BF16).reshape(16, 16, CHANNELS)


def place_of(share):
    return (share // 3, share % 3) if share < 30 else (10, 2 * (share - 30))


def share_kernel(parts, token, shares):
    for tile in reversed(range(TILES)):
        total = jnp.sum(parts[:, tile, :, :].astype(F32), axis=0)
        if tile == TILES - 1:
            sums = total[8:9] + total[9:10] + total[10:11]
            pieces = split(sums)[:2]
            lines = [piece[:, 128 * m : 128 * m + 128] for piece in pieces for m in range(3)]
            block = stack_lines(lines, 8)
        for share in range(32):
            if place_of(share)[0] == tile:
                third = place_of(share)[1]
                mine = total[:, 128 * third : 128 * third + 128]
                shares[share, :, :] = jnp.concatenate([mine, block], axis=0).astype(BF16)


def own_kernel(parts, mine, sums):
    total = jnp.sum(parts[...].astype(F32), axis=0)
    for i in range(mine.shape[0]):
        mine[i, :, :] = total[0:16].astype(BF16)
    lines = total[16:19] + total[19:22]
    sums[...] = jnp.concatenate([lines[0:1], lines[1:2], lines[2:3]], axis=1)


def finish_kernel(
    counts, sums, other, stats, film, action, held, kept_at, grad_film, grad_inputs, kept, done,
):
    copy = pltpu.make_async_copy(kept_at, kept, done.at[0])
    copy.start()
    total = sums[...] + other[...]
    scale_grad, shift_grad = total[:, :CHANNELS], total[:, CHANNELS:]
    cells, mean, inverse, scale, shift = norm_terms(stats, film)
    grad_film[:, :CHANNELS] = action[...] * scale_grad
    grad_film[:, CHANNELS:] = action[...] * shift_grad
    swap = swap_matrix(None)
    live = (iota((256, 1), 0) & 15) < counts[0]
    copy.wait()
    for g in range(4):
        part = slice(16 * g, 16 * g + 16)
        x = held[part, :, :].reshape(256, CHANNELS).astype(F32)
        normed = (x - mean) * inverse
        value = kept[256 * g : 256 * g + 256, :] - inverse * (
            scale * shift_grad / cells + normed * scale * scale_grad / cells
        )
        value = jnp.where(live, value, 0.0).astype(BF16)
        grad_inputs[:, part, :] = dot(swap, value).astype(BF16).reshape(16, 16, CHANNELS)


def unpack_kernel(tiles, grad_weight):
    zero = jnp.zeros((16, 128), BF16)
    thirds = [
        jnp.concatenate([tiles[3 * u + n] for u in range(10)] + [last], axis=0)
        for n, last in enumerate((tiles[30], zero, tiles[31]))
    ]
    even = jnp.concatenate([thirds[0], thirds[2][:, :64]], axis=1)
    odd = jnp.concatenate([thirds[1], thirds[2][:, 64:]], axis=1)
    row, col = iota((384, 352), 0), iota((384, 352), 1)
    k = row & 31
    chosen = (k < 27) & (col == (row >> 5) + 12 * (k >> 1) + 176 * (k & 1))
    chosen = jnp.where(chosen, 1.0, 0.0).astype(BF16)
    found = dot(chosen, jnp.concatenate([even, odd], axis=0)).reshape(12, 32, CHANNELS)
    grad_weight[...] = found[:, :27, :]


SMEM = pl.BlockSpec(memory_space=pltpu.SMEM)
VMEM = pl.BlockSpec(memory_space=pltpu.VMEM)
ANY = pl.BlockSpec(memory_space=pl.ANY)


def call(kernel, scalars, arrays, outs, scratch=(), flops=0, name=None, left=0, room=12, copies=0):
    split_at = len(arrays) - left
    arrays = list(arrays[:split_at]) + [
        pltpu.with_memory_space_constraint(x, pltpu.HBM) for x in arrays[split_at:]
    ]
    moved = sum(x.size * x.dtype.itemsize for x in arrays)
    shapes, specs = [], []
    for shape, dtype, *marked in outs:
        moved += math.prod(shape) * jnp.dtype(dtype).itemsize
        shapes.append(pltpu.HBM(shape, dtype) if marked else jax.ShapeDtypeStruct(shape, dtype))
        specs.append(ANY if marked else VMEM)
    return pl.pallas_call(
        kernel,
        out_shape=shapes,
        in_specs=[SMEM] * len(scalars) + [VMEM] * split_at + [ANY] * left,
        out_specs=specs,
        scratch_shapes=[pltpu.VMEM(*s) for s in scratch]
        + ([pltpu.SemaphoreType.DMA((copies,))] if copies else []),
        compiler_params=pltpu.CompilerParams(vmem_limit_bytes=room * MIB),
        cost_estimate=pl.CostEstimate(flops=flops, bytes_accessed=moved, transcendentals=0),
        name=name,
    )(*scalars, *arrays)


def exchange(array, axis, groups=None):
    return lax.all_to_all(array, axis, 0, 0, axis_index_groups=groups, tiled=True)


def body(features, cotangent, counts, neighbours, send_x, send_y, action, conv_weight, film_weight):
    size_x, size_y = lax.axis_size("gx"), lax.axis_size("gy")
    count = counts.reshape(1)
    rule = neighbours[0, 0]
    list_x = pltpu.with_memory_space_constraint(send_x[0, 0], pltpu.HBM)
    block = ((VOXELS, 16, CHANNELS), BF16)
    face = ((16, 16, CHANNELS), BF16)
    spaced = ((6, 6, 6, 16, CHANNELS), BF16)
    joined = ((16, 16, 384), BF16)
    held, up, stats, face_low, face_high, film = call(
        pack_kernel,
        [count, list_x],
        [features[0, 0], cotangent[0, 0], film_weight, action[None]],
        [block, block, ((size_x, 4, 128), F32), face, face, ((1, 2 * CHANNELS), F32)],
        [((SLOTS, VOXELS, CHANNELS), BF16), ((SLOTS, VOXELS, CHANNELS), BF16), ((128, 2 * CHANNELS), F32), ((1, 128), F32)],
        flops=10**9,
        name="pack",
        left=4,
        copies=4,
    )
    up_x = [(i, i + 1) for i in range(size_x - 1)]
    down_x = [(i + 1, i) for i in range(size_x - 1)]
    up_y = [(i, i + 1) for i in range(size_y - 1)]
    down_y = [(i + 1, i) for i in range(size_y - 1)]
    lower = lax.ppermute(face_high, "gx", up_x)
    upper = lax.ppermute(face_low, "gx", down_x)
    stats = exchange(stats, "gx")
    weight = jnp.transpose(conv_weight, (1, 0, 2))
    face_low, face_high, stats = call(
        cross_kernel,
        [send_y[0, 0]],
        [held, up, lower, upper, stats],
        [joined, joined, ((size_y, 4, 128), F32)],
        flops=10**8,
        name="cross",
    )
    side_l = lax.ppermute(face_high, "gy", up_y)
    side_u = lax.ppermute(face_low, "gy", down_y)
    stats = exchange(stats, "gy")
    core = lax.axis_index("gx") & 1
    swapped = [(i, i ^ 1) for i in range(size_x)]
    taps = ((27, CHANNELS, CHANNELS), BF16)
    total = ((1024, CHANNELS), F32)
    raw, back, turned = call(
        early_kernel,
        [],
        [held, up, lower, upper, side_l, side_u, rule, weight],
        [(*spaced, True), total, ((CHANNELS, 1024), BF16)],
        [spaced, spaced, face, face, taps],
        flops=3 * 10**9,
        name="early",
        left=1,
        copies=2,
        room=20,
    )
    half = ((8, TILES, 16, 384), BF16)
    near, far, padded = call(
        weight_kernel,
        [count, core.reshape(1)],
        [turned, rule, stats, film, raw],
        [half, half, (*spaced, True)],
        [spaced, spaced, ((4, 256, 1024), BF16)],
        flops=4 * 10**9,
        name="weight",
        left=1,
        copies=2,
        room=20,
    )
    other = lax.ppermute(far, "gx", swapped)
    kept, lines = call(
        slope_kernel,
        [count],
        [held, up, back, stats, film],
        [(*total, True), ((16, 384), F32)],
        [total],
        flops=10**8,
        name="slope",
        copies=1,
    )
    tile = lax.broadcasted_iota(jnp.int32, half[0], 1)
    row = lax.broadcasted_iota(jnp.int32, half[0], 2)
    parts = near.astype(F32) + other.astype(F32)
    parts = jnp.where((tile == TILES - 1) & (row >= 8), lines, parts).astype(BF16)
    parts = exchange(parts, "gx", [list(range(c, size_x, 2)) for c in range(2)])
    output, token = call(
        forward_kernel,
        [count],
        [held, weight, padded],
        [((SLOTS, VOXELS, CHANNELS), BF16), ((8, 128), F32)],
        [total, taps, spaced],
        flops=3 * 10**9,
        name="forward",
        left=2,
        copies=2,
        room=16,
    )
    (shares,) = call(share_kernel, [], [parts, token], [((size_y, 24, 128), BF16)], name="share")
    shares = exchange(shares, "gy")
    mine, sums = call(
        own_kernel, [], [shares], [((size_y, 16, 128), BF16), ((1, 2 * CHANNELS), F32)], name="own"
    )
    other = lax.ppermute(sums, "gx", swapped)
    tiles = exchange(mine, "gy")
    grad_film, grad_inputs = call(
        finish_kernel,
        [count],
        [sums, other, stats, film, action[:, None], held, kept],
        [((128, 2 * CHANNELS), F32), ((SLOTS, VOXELS, CHANNELS), BF16)],
        [total],
        flops=10**9,
        name="finish",
        left=1,
        copies=1,
    )
    (grad_weight,) = call(unpack_kernel, [], [tiles], [((12, 27, CHANNELS), F32)], name="unpack")
    return output[None, None], grad_inputs[None, None], grad_weight, grad_film


def solution(mesh):
    tile = P("gx", "gy")
    return jax.shard_map(
        body,
        mesh=mesh,
        in_specs=(tile, tile, tile, tile, tile, tile, P(), P(), P()),
        out_specs=(tile, tile, P("gx"), P()),
        check_vma=False,
    )
```

```python
import math

import jax
import jax.numpy as jnp
from jax import lax
from jax.experimental import pallas as pl
from jax.experimental.pallas import tpu as pltpu
from jax.sharding import PartitionSpec as P

SLOTS = 16
VOXELS = 64
CHANNELS = 192
TILES = 11
MIB = 1024 * 1024
F32 = jnp.float32
BF16 = jnp.bfloat16


def iota(shape, dim):
    return lax.broadcasted_iota(jnp.int32, shape, dim)


def dot(left, right):
    return jnp.dot(left, right, preferred_element_type=F32)


def dot_nt(left, right):
    return lax.dot_general(left, right, (((1,), (1,)), ((), ())), preferred_element_type=F32)


def swap_matrix(count):
    row, col = iota((256, 256), 0), iota((256, 256), 1)
    hit = ((row >> 4) == (col & 15)) & ((row & 15) == (col >> 4))
    if count is not None:
        hit = hit & ((row & 15) < count)
    return jnp.where(hit, 1.0, 0.0).astype(BF16)


def list_column(ref, side, length, rows, half):
    row = iota((rows, 1), 0)
    entry = jnp.full((rows, 1), -1, jnp.int32)
    for e in range(length):
        value = ref[side, e]
        entry = jnp.where((row == e) | (row == e + half), value, entry)
    return entry


def pick(column, width, low, high, base, second, half):
    rows = column.shape[0]
    row, col = iota((rows, width), 0), iota((rows, width), 1)
    target = column - low + base + jnp.where(row >= half, second, 0)
    hit = (column >= low) & (column < high) & (col == target)
    return jnp.where(hit, 1.0, 0.0).astype(BF16)


def pack_lines(first, second):
    rest = jnp.concatenate([first[:, 128:], second[:, 128:]], axis=1)
    return [first[:, :128], second[:, :128], rest]


def unpack_lines(lines):
    first = jnp.concatenate([lines[0:1], lines[2:3, :64]], axis=1)
    second = jnp.concatenate([lines[1:2], lines[2:3, 64:]], axis=1)
    return first, second


def stack_lines(lines, rows):
    row = iota((rows, 128), 0)
    block = jnp.zeros((rows, 128), F32)
    for e, line in enumerate(lines):
        block = jnp.where(row == e, line, block)
    return block


def join_fields(value):
    first, second = value[0:16], value[16:32]
    rest = jnp.concatenate([first[:, 128:], second[:, 128:]], axis=1)
    return jnp.concatenate([first[:, :128], second[:, :128], rest], axis=1).astype(BF16)


def one_field(joined, which):
    tail = joined[..., 256:320] if which == 0 else joined[..., 320:384]
    return jnp.concatenate([joined[..., 128 * which : 128 * which + 128], tail], axis=-1)


def pack_kernel(
    counts, send_x, feat_at, cot_at, film_at, action_at,
    held, up, stats, face_low, face_high, film, feat, cot, film_weight, action, done,
):
    pairs = ((feat_at, feat), (cot_at, cot), (film_at, film_weight), (action_at, action))
    copies = [
        pltpu.make_async_copy(source, target, done.at[n]) for n, (source, target) in enumerate(pairs)
    ]
    for copy in copies:
        copy.start()
    swap = swap_matrix(counts[0])
    for copy in copies:
        copy.wait()
    total = jnp.zeros((1, CHANNELS), F32)
    square = jnp.zeros((1, CHANNELS), F32)
    for g in range(4):
        part = slice(16 * g, 16 * g + 16)
        moved = dot(swap, feat[:, part, :].reshape(256, CHANNELS))
        total += jnp.sum(moved, axis=0, keepdims=True)
        square += jnp.sum(moved * moved, axis=0, keepdims=True)
        held[part, :, :] = moved.astype(BF16).reshape(16, 16, CHANNELS)
        moved = dot(swap, cot[:, part, :].reshape(256, CHANNELS))
        up[part, :, :] = moved.astype(BF16).reshape(16, 16, CHANNELS)
    cells = (counts[0] * VOXELS).astype(F32)
    block = stack_lines(pack_lines(total, square) + [cells], 4)
    for i in range(stats.shape[0]):
        stats[i, :, :] = block
    for side in range(2):
        chosen = pick(list_column(send_x, side, 8, 16, 8), 32, 0, SLOTS, 0, 16, 8)
        for i in range(16):
            both = jnp.concatenate([held[48 * side + i], up[48 * side + i]], axis=0)
            target = (face_low, face_high)[side]
            target[i, :, :] = dot(chosen, both).astype(BF16)
    film[...] = lax.dot_general(
        action[...],
        film_weight[...],
        (((1,), (0,)), ((), ())),
        precision=lax.Precision.HIGHEST,
        preferred_element_type=F32,
    )


def cross_kernel(send_y, held, up, lower, upper, stats, face_low, face_high, spread):
    block = jnp.sum(stats[...], axis=0)
    for i in range(spread.shape[0]):
        spread[i, :, :] = block
    for side in range(2):
        target = (face_low, face_high)[side]
        column = list_column(send_y, side, 12, 32, 16)
        local = pick(column, 32, 0, SLOTS, 0, 16, 16)
        from_lower = pick(column, 16, 17, 25, 0, 8, 16)
        from_upper = pick(column, 16, 25, 33, 0, 8, 16)
        for a in range(4):
            for c in range(4):
                v = 16 * a + 12 * side + c
                value = dot(local, jnp.concatenate([held[v], up[v]], axis=0))
                if a == 3:
                    value += dot(from_lower, lower[12 * side + c])
                if a == 0:
                    value += dot(from_upper, upper[12 * side + c])
                target[4 * a + c, :, :] = join_fields(value)


def norm_terms(stats, film):
    lines = jnp.sum(stats[...], axis=0)
    total, square = unpack_lines(lines)
    cells = lines[3:4, 0:1]
    mean = total / cells
    variance = square / cells - mean * mean
    inverse = lax.rsqrt(variance + 1e-05)
    scale = 1.0 + film[:, :CHANNELS]
    shift = film[:, CHANNELS:]
    return cells, mean, inverse, scale, shift


def gather_blocks(rule, half, own, low, high, low_y, high_y, padded):
    entries = rule[...]
    col = iota((16, 80), 1)
    hot = []
    for n in range(27):
        column = entries[:, n : n + 1]
        target = jnp.where(column >= 17, column - 1 + half, column)
        target = jnp.where(column >= 25, column + 7 + half, target)
        target = jnp.where(column >= 33, column + 15, target)
        target = jnp.where(column >= 45, column + 19, target)
        hit = (column != 16) & (col == target)
        hot.append(jnp.where(hit, 1.0, 0.0).astype(BF16))
    none = jnp.zeros((16, CHANNELS), BF16)
    for a in range(4):
        for b in range(4):
            for c in range(4):
                mine = own[16 * a + 4 * b + c]
                padded[a + 1, b + 1, c + 1, :, :] = mine
                ways = [
                    [(q + 1, 0)] + ([(5, 1)] if q == 0 else []) + ([(0, -1)] if q == 3 else [])
                    for q in (a, b, c)
                ]
                places = [(x, y, z) for x in ways[0] for y in ways[1] for z in ways[2]][1:]
                if not places:
                    continue
                listed = jnp.concatenate(
                    [
                        mine,
                        low[4 * b + c] if a == 3 else none,
                        high[4 * b + c] if a == 0 else none,
                        low_y[4 * a + c] if b == 3 else none,
                        high_y[4 * a + c] if b == 0 else none,
                    ],
                    axis=0,
                )
                chosen = jnp.concatenate(
                    [hot[9 * (x[1] + 1) + 3 * (y[1] + 1) + z[1] + 1] for x, y, z in places], axis=0
                )
                found = dot(chosen, listed).astype(BF16)
                for m, (x, y, z) in enumerate(places):
                    padded[x[0], y[0], z[0], :, :] = found[16 * m : 16 * m + 16]


def window(padded, k):
    x, y, z = k // 9, (k // 3) % 3, k % 3
    part = padded[pl.ds(x, 4), pl.ds(y, 4), pl.ds(z, 4), :, :]
    return part.reshape(1024, CHANNELS)


def early_kernel(
    up, lower, upper, side_l, side_u, rule, weight_at,
    back, turned, wide, low_y, high_y, weight, done,
):
    copy = pltpu.make_async_copy(weight_at, weight, done.at[0])
    copy.start()
    low_y[...] = one_field(side_l[...], 1)
    high_y[...] = one_field(side_u[...], 1)
    gather_blocks(rule, 8, up, lower, upper, low_y, high_y, wide)
    same = jnp.where(iota((CHANNELS, CHANNELS), 0) == iota((CHANNELS, CHANNELS), 1), 1.0, 0.0)
    turned[...] = dot_nt(same.astype(BF16), up[...].reshape(1024, CHANNELS)).astype(BF16)
    back[...] = jnp.zeros_like(back)
    copy.wait()

    def step(t, carry):
        k = 3 * t
        total = dot(window(wide, k), weight[26 - k])
        total += dot(window(wide, k + 1), weight[25 - k])
        back[...] += total + dot(window(wide, k + 2), weight[24 - k])
        return carry

    lax.fori_loop(0, 9, step, 0)


def weight_kernel(
    counts, core, held, lower, upper, side_l, side_u, up_turned, rule, stats, film,
    near, far, padded_at, hid, low, high, low_y, high_y, padded, turned, done,
):
    cells, mean, inverse, scale, shift = norm_terms(stats, film)
    row, col = iota((256, CHANNELS), 0), iota((256, CHANNELS), 1)
    group = ((row >> 4) & 7) * 2 + jnp.where(row >= 128, 1 - core[0], core[0])
    for m in range(4):
        place = (row + 4 * m) & 15
        spread = (place < 12) & (col == group * 12 + place)
        spread = jnp.where(spread, 1.0, 0.0).astype(BF16)
        turned[m, :, :] = dot(spread, up_turned[...]).astype(BF16)

    def act(x):
        x = (x.astype(F32) - mean) * inverse * scale + shift
        return jnp.maximum(x, 0.0)

    live = (iota((256, 1), 0) & 15) < counts[0]
    for g in range(4):
        part = slice(16 * g, 16 * g + 16)
        x = act(held[part, :, :].reshape(256, CHANNELS))
        hid[part, :, :] = jnp.where(live, x, 0.0).astype(BF16).reshape(16, 16, CHANNELS)
    for source, target in (
        (lower[...], low),
        (upper[...], high),
        (one_field(side_l[...], 0), low_y),
        (one_field(side_u[...], 0), high_y),
    ):
        x = act(source.reshape(256, CHANNELS))
        target[...] = x.astype(BF16).reshape(16, 16, CHANNELS)
    gather_blocks(rule, 0, hid, low, high, low_y, high_y, padded)
    out = pltpu.make_async_copy(padded, padded_at, done.at[0])
    out.start()
    line = iota((256, 384), 0) & 15

    def pair(m, k1, k2):
        grad1 = dot(turned[m], window(padded, k1))
        grad2 = dot(turned[m], window(padded, k2)) if k2 is not None else jnp.zeros_like(grad1)
        rest = jnp.concatenate([grad1[:, 128:], grad2[:, 128:]], axis=1)
        return jnp.concatenate([grad1[:, :128], grad2[:, :128], rest], axis=1)

    def store(at, value):
        value = value.astype(BF16).reshape(16, 1, 16, 384)
        near[:, pl.ds(at, 1), :, :] = value[:8]
        far[:, pl.ds(at, 1), :, :] = value[8:]

    def step(q, carry):
        k = 8 * q
        first, second = pair(0, k, k + 1), pair(1, k + 2, k + 3)
        store(3 * q, jnp.where(line < 12, first, second))
        third = pair(2, k + 4, k + 5)
        store(3 * q + 1, jnp.where(line < 8, second, third))
        fourth = pair(3, k + 6, k + 7)
        store(3 * q + 2, jnp.where(line < 4, third, fourth))
        return carry

    lax.fori_loop(0, 3, step, 0)
    first, second = pair(0, 24, 25), pair(1, 26, None)
    store(9, jnp.where(line < 12, first, second))
    store(10, jnp.where(line < 8, second, 0.0))
    out.wait()


def split(value):
    first = value.astype(BF16).astype(F32)
    second = (value - first).astype(BF16).astype(F32)
    return first, second, value - first - second


def slope_kernel(counts, held, up, back, stats, film, kept_at, lines, kept, done):
    cells, mean, inverse, scale, shift = norm_terms(stats, film)
    shift_grad = jnp.zeros((1, CHANNELS), F32)
    scale_grad = jnp.zeros((1, CHANNELS), F32)
    live = (iota((256, 1), 0) & 15) < counts[0]
    for g in range(4):
        at = slice(256 * g, 256 * g + 256)
        part = slice(16 * g, 16 * g + 16)
        x = held[part, :, :].reshape(256, CHANNELS).astype(F32)
        normed = (x - mean) * inverse
        slope = jnp.where(live & (normed * scale + shift > 0), back[at, :], 0.0)
        shift_grad += jnp.sum(slope, axis=0, keepdims=True)
        scale_grad += jnp.sum(slope * normed, axis=0, keepdims=True)
        kept[at, :] = up[part, :, :].reshape(256, CHANNELS).astype(F32) + inverse * (slope * scale)
    out = pltpu.make_async_copy(kept, kept_at, done.at[0])
    out.start()
    row = iota((16, 384), 0)
    block = jnp.zeros((16, 384), F32)
    for e, piece in enumerate(split(jnp.concatenate([scale_grad, shift_grad], axis=1))):
        block = jnp.where(row == 8 + e, piece, block)
    lines[...] = block
    out.wait()


def forward_kernel(
    counts, held, weight_at, padded_at, output, token, acc, weight, padded, done,
):
    token[...] = jnp.zeros_like(token)
    copies = [
        pltpu.make_async_copy(weight_at, weight, done.at[0]),
        pltpu.make_async_copy(padded_at, padded, done.at[1]),
    ]
    for copy in copies:
        copy.start()
    acc[...] = jnp.zeros_like(acc)
    for copy in copies:
        copy.wait()

    def step(t, carry):
        k = 3 * t
        total = dot_nt(window(padded, k), weight[k])
        total += dot_nt(window(padded, k + 1), weight[k + 1])
        acc[...] += total + dot_nt(window(padded, k + 2), weight[k + 2])
        return carry

    lax.fori_loop(0, 9, step, 0)
    swap = swap_matrix(None)
    live = (iota((256, 1), 0) & 15) < counts[0]
    for g in range(4):
        part = slice(16 * g, 16 * g + 16)
        x = held[part, :, :].reshape(256, CHANNELS).astype(F32)
        mixed = jnp.where(live, x + acc[256 * g : 256 * g + 256, :], 0.0).astype(BF16)
        output[:, part, :] = dot(swap, mixed).astype(BF16).reshape(16, 16, CHANNELS)


def place_of(share):
    return (share // 3, share % 3) if share < 30 else (10, 2 * (share - 30))


def share_kernel(parts, token, shares):
    for tile in reversed(range(TILES)):
        total = jnp.sum(parts[:, tile, :, :].astype(F32), axis=0)
        if tile == TILES - 1:
            sums = total[8:9] + total[9:10] + total[10:11]
            pieces = split(sums)[:2]
            lines = [piece[:, 128 * m : 128 * m + 128] for piece in pieces for m in range(3)]
            block = stack_lines(lines, 8)
        for share in range(32):
            if place_of(share)[0] == tile:
                third = place_of(share)[1]
                mine = total[:, 128 * third : 128 * third + 128]
                shares[share, :, :] = jnp.concatenate([mine, block], axis=0).astype(BF16)


def own_kernel(parts, mine, sums):
    total = jnp.sum(parts[...].astype(F32), axis=0)
    for i in range(mine.shape[0]):
        mine[i, :, :] = total[0:16].astype(BF16)
    lines = total[16:19] + total[19:22]
    sums[...] = jnp.concatenate([lines[0:1], lines[1:2], lines[2:3]], axis=1)


def finish_kernel(
    counts, sums, other, stats, film, action, held, kept_at, grad_film, grad_inputs, kept, done,
):
    copy = pltpu.make_async_copy(kept_at, kept, done.at[0])
    copy.start()
    total = sums[...] + other[...]
    scale_grad, shift_grad = total[:, :CHANNELS], total[:, CHANNELS:]
    cells, mean, inverse, scale, shift = norm_terms(stats, film)
    grad_film[:, :CHANNELS] = action[...] * scale_grad
    grad_film[:, CHANNELS:] = action[...] * shift_grad
    swap = swap_matrix(None)
    live = (iota((256, 1), 0) & 15) < counts[0]
    copy.wait()
    for g in range(4):
        part = slice(16 * g, 16 * g + 16)
        x = held[part, :, :].reshape(256, CHANNELS).astype(F32)
        normed = (x - mean) * inverse
        value = kept[256 * g : 256 * g + 256, :] - inverse * (
            scale * shift_grad / cells + normed * scale * scale_grad / cells
        )
        value = jnp.where(live, value, 0.0).astype(BF16)
        grad_inputs[:, part, :] = dot(swap, value).astype(BF16).reshape(16, 16, CHANNELS)


def unpack_kernel(tiles, grad_weight):
    zero = jnp.zeros((16, 128), BF16)
    thirds = [
        jnp.concatenate([tiles[3 * u + n] for u in range(10)] + [last], axis=0)
        for n, last in enumerate((tiles[30], zero, tiles[31]))
    ]
    even = jnp.concatenate([thirds[0], thirds[2][:, :64]], axis=1)
    odd = jnp.concatenate([thirds[1], thirds[2][:, 64:]], axis=1)
    row, col = iota((384, 352), 0), iota((384, 352), 1)
    k = row & 31
    chosen = (k < 27) & (col == (row >> 5) + 12 * (k >> 1) + 176 * (k & 1))
    chosen = jnp.where(chosen, 1.0, 0.0).astype(BF16)
    found = dot(chosen, jnp.concatenate([even, odd], axis=0)).reshape(12, 32, CHANNELS)
    grad_weight[...] = found[:, :27, :]


SMEM = pl.BlockSpec(memory_space=pltpu.SMEM)
VMEM = pl.BlockSpec(memory_space=pltpu.VMEM)
ANY = pl.BlockSpec(memory_space=pl.ANY)


def call(kernel, scalars, arrays, outs, scratch=(), flops=0, name=None, left=0, room=12, copies=0):
    split_at = len(arrays) - left
    arrays = list(arrays[:split_at]) + [
        pltpu.with_memory_space_constraint(x, pltpu.HBM) for x in arrays[split_at:]
    ]
    moved = sum(x.size * x.dtype.itemsize for x in arrays)
    shapes, specs = [], []
    for shape, dtype, *marked in outs:
        moved += math.prod(shape) * jnp.dtype(dtype).itemsize
        shapes.append(pltpu.HBM(shape, dtype) if marked else jax.ShapeDtypeStruct(shape, dtype))
        specs.append(ANY if marked else VMEM)
    return pl.pallas_call(
        kernel,
        out_shape=shapes,
        in_specs=[SMEM] * len(scalars) + [VMEM] * split_at + [ANY] * left,
        out_specs=specs,
        scratch_shapes=[pltpu.VMEM(*s) for s in scratch]
        + ([pltpu.SemaphoreType.DMA((copies,))] if copies else []),
        compiler_params=pltpu.CompilerParams(vmem_limit_bytes=room * MIB),
        cost_estimate=pl.CostEstimate(flops=flops, bytes_accessed=moved, transcendentals=0),
        name=name,
    )(*scalars, *arrays)


def exchange(array, axis, groups=None):
    return lax.all_to_all(array, axis, 0, 0, axis_index_groups=groups, tiled=True)


def body(features, cotangent, counts, neighbours, send_x, send_y, action, conv_weight, film_weight):
    size_x, size_y = lax.axis_size("gx"), lax.axis_size("gy")
    count = counts.reshape(1)
    rule = neighbours[0, 0]
    list_x = pltpu.with_memory_space_constraint(send_x[0, 0], pltpu.HBM)
    block = ((VOXELS, 16, CHANNELS), BF16)
    face = ((16, 16, CHANNELS), BF16)
    spaced = ((6, 6, 6, 16, CHANNELS), BF16)
    joined = ((16, 16, 384), BF16)
    held, up, stats, face_low, face_high, film = call(
        pack_kernel,
        [count, list_x],
        [features[0, 0], cotangent[0, 0], film_weight, action[None]],
        [block, block, ((size_x, 4, 128), F32), face, face, ((1, 2 * CHANNELS), F32)],
        [((SLOTS, VOXELS, CHANNELS), BF16), ((SLOTS, VOXELS, CHANNELS), BF16), ((128, 2 * CHANNELS), F32), ((1, 128), F32)],
        flops=10**9,
        name="pack",
        left=4,
        copies=4,
    )
    up_x = [(i, i + 1) for i in range(size_x - 1)]
    down_x = [(i + 1, i) for i in range(size_x - 1)]
    up_y = [(i, i + 1) for i in range(size_y - 1)]
    down_y = [(i + 1, i) for i in range(size_y - 1)]
    lower = lax.ppermute(face_high, "gx", up_x)
    upper = lax.ppermute(face_low, "gx", down_x)
    stats = exchange(stats, "gx")
    weight = jnp.transpose(conv_weight, (1, 0, 2))
    face_low, face_high, stats = call(
        cross_kernel,
        [send_y[0, 0]],
        [held, up, lower, upper, stats],
        [joined, joined, ((size_y, 4, 128), F32)],
        flops=10**8,
        name="cross",
    )
    side_l = lax.ppermute(face_high, "gy", up_y)
    side_u = lax.ppermute(face_low, "gy", down_y)
    stats = exchange(stats, "gy")
    core = lax.axis_index("gx") & 1
    swapped = [(i, i ^ 1) for i in range(size_x)]
    taps = ((27, CHANNELS, CHANNELS), BF16)
    total = ((1024, CHANNELS), F32)
    back, turned = call(
        early_kernel,
        [],
        [up, lower, upper, side_l, side_u, rule, weight],
        [total, ((CHANNELS, 1024), BF16)],
        [spaced, face, face, taps],
        flops=3 * 10**9,
        name="early",
        left=1,
        copies=1,
        room=20,
    )
    half = ((8, TILES, 16, 384), BF16)
    near, far, padded = call(
        weight_kernel,
        [count, core.reshape(1)],
        [held, lower, upper, side_l, side_u, turned, rule, stats, film],
        [half, half, (*spaced, True)],
        [block, face, face, face, face, spaced, ((4, 256, 1024), BF16)],
        flops=4 * 10**9,
        name="weight",
        copies=1,
        room=20,
    )
    other = lax.ppermute(far, "gx", swapped)
    kept, lines = call(
        slope_kernel,
        [count],
        [held, up, back, stats, film],
        [(*total, True), ((16, 384), F32)],
        [total],
        flops=10**8,
        name="slope",
        copies=1,
    )
    tile = lax.broadcasted_iota(jnp.int32, half[0], 1)
    row = lax.broadcasted_iota(jnp.int32, half[0], 2)
    parts = near.astype(F32) + other.astype(F32)
    parts = jnp.where((tile == TILES - 1) & (row >= 8), lines, parts).astype(BF16)
    parts = exchange(parts, "gx", [list(range(c, size_x, 2)) for c in range(2)])
    output, token = call(
        forward_kernel,
        [count],
        [held, weight, padded],
        [((SLOTS, VOXELS, CHANNELS), BF16), ((8, 128), F32)],
        [total, taps, spaced],
        flops=3 * 10**9,
        name="forward",
        left=2,
        copies=2,
        room=16,
    )
    (shares,) = call(share_kernel, [], [parts, token], [((size_y, 24, 128), BF16)], name="share")
    shares = exchange(shares, "gy")
    mine, sums = call(
        own_kernel, [], [shares], [((size_y, 16, 128), BF16), ((1, 2 * CHANNELS), F32)], name="own"
    )
    other = lax.ppermute(sums, "gx", swapped)
    tiles = exchange(mine, "gy")
    grad_film, grad_inputs = call(
        finish_kernel,
        [count],
        [sums, other, stats, film, action[:, None], held, kept],
        [((128, 2 * CHANNELS), F32), ((SLOTS, VOXELS, CHANNELS), BF16)],
        [total],
        flops=10**9,
        name="finish",
        left=1,
        copies=1,
    )
    (grad_weight,) = call(unpack_kernel, [], [tiles], [((12, 27, CHANNELS), F32)], name="unpack")
    return output[None, None], grad_inputs[None, None], grad_weight, grad_film


def solution(mesh):
    tile = P("gx", "gy")
    return jax.shard_map(
        body,
        mesh=mesh,
        in_specs=(tile, tile, tile, tile, tile, tile, P(), P(), P()),
        out_specs=(tile, tile, P("gx"), P()),
        check_vma=False,
    )
```

```python
import math

import jax
import jax.numpy as jnp
from jax import lax
from jax.experimental import pallas as pl
from jax.experimental.pallas import tpu as pltpu
from jax.sharding import PartitionSpec as P

SLOTS = 16
VOXELS = 64
CHANNELS = 192
TILES = 11
MIB = 1024 * 1024
F32 = jnp.float32
BF16 = jnp.bfloat16


def iota(shape, dim):
    return lax.broadcasted_iota(jnp.int32, shape, dim)


def dot(left, right):
    return jnp.dot(left, right, preferred_element_type=F32)


def dot_nt(left, right):
    return lax.dot_general(left, right, (((1,), (1,)), ((), ())), preferred_element_type=F32)


def swap_matrix(count):
    row, col = iota((256, 256), 0), iota((256, 256), 1)
    hit = ((row >> 4) == (col & 15)) & ((row & 15) == (col >> 4))
    if count is not None:
        hit = hit & ((row & 15) < count)
    return jnp.where(hit, 1.0, 0.0).astype(BF16)


def list_column(ref, side, length, rows, half):
    row = iota((rows, 1), 0)
    entry = jnp.full((rows, 1), -1, jnp.int32)
    for e in range(length):
        value = ref[side, e]
        entry = jnp.where((row == e) | (row == e + half), value, entry)
    return entry


def pick(column, width, low, high, base, second, half):
    rows = column.shape[0]
    row, col = iota((rows, width), 0), iota((rows, width), 1)
    target = column - low + base + jnp.where(row >= half, second, 0)
    hit = (column >= low) & (column < high) & (col == target)
    return jnp.where(hit, 1.0, 0.0).astype(BF16)


def pack_lines(first, second):
    rest = jnp.concatenate([first[:, 128:], second[:, 128:]], axis=1)
    return [first[:, :128], second[:, :128], rest]


def unpack_lines(lines):
    first = jnp.concatenate([lines[0:1], lines[2:3, :64]], axis=1)
    second = jnp.concatenate([lines[1:2], lines[2:3, 64:]], axis=1)
    return first, second


def stack_lines(lines, rows):
    row = iota((rows, 128), 0)
    block = jnp.zeros((rows, 128), F32)
    for e, line in enumerate(lines):
        block = jnp.where(row == e, line, block)
    return block


def join_fields(value):
    first, second = value[0:16], value[16:32]
    rest = jnp.concatenate([first[:, 128:], second[:, 128:]], axis=1)
    return jnp.concatenate([first[:, :128], second[:, :128], rest], axis=1).astype(BF16)


def one_field(joined, which):
    tail = joined[..., 256:320] if which == 0 else joined[..., 320:384]
    return jnp.concatenate([joined[..., 128 * which : 128 * which + 128], tail], axis=-1)


def pack_kernel(
    counts, send_x, feat_at, cot_at, held, up, stats, face_low, face_high, feat, cot, done,
):
    pairs = ((feat_at, feat), (cot_at, cot))
    copies = [
        pltpu.make_async_copy(source, target, done.at[n]) for n, (source, target) in enumerate(pairs)
    ]
    for copy in copies:
        copy.start()
    swap = swap_matrix(counts[0])
    for copy in copies:
        copy.wait()
    total = jnp.zeros((1, CHANNELS), F32)
    square = jnp.zeros((1, CHANNELS), F32)
    for g in range(4):
        part = slice(16 * g, 16 * g + 16)
        moved = dot(swap, feat[:, part, :].reshape(256, CHANNELS))
        total += jnp.sum(moved, axis=0, keepdims=True)
        square += jnp.sum(moved * moved, axis=0, keepdims=True)
        held[part, :, :] = moved.astype(BF16).reshape(16, 16, CHANNELS)
        moved = dot(swap, cot[:, part, :].reshape(256, CHANNELS))
        up[part, :, :] = moved.astype(BF16).reshape(16, 16, CHANNELS)
    cells = (counts[0] * VOXELS).astype(F32)
    block = stack_lines(pack_lines(total, square) + [cells], 4)
    for i in range(stats.shape[0]):
        stats[i, :, :] = block
    for side in range(2):
        chosen = pick(list_column(send_x, side, 8, 16, 8), 32, 0, SLOTS, 0, 16, 8)
        for i in range(16):
            both = jnp.concatenate([held[48 * side + i], up[48 * side + i]], axis=0)
            target = (face_low, face_high)[side]
            target[i, :, :] = dot(chosen, both).astype(BF16)


def cross_kernel(send_y, held, up, lower, upper, stats, face_low, face_high, spread):
    block = jnp.sum(stats[...], axis=0)
    for i in range(spread.shape[0]):
        spread[i, :, :] = block
    for side in range(2):
        target = (face_low, face_high)[side]
        column = list_column(send_y, side, 12, 32, 16)
        local = pick(column, 32, 0, SLOTS, 0, 16, 16)
        from_lower = pick(column, 16, 17, 25, 0, 8, 16)
        from_upper = pick(column, 16, 25, 33, 0, 8, 16)
        for a in range(4):
            for c in range(4):
                v = 16 * a + 12 * side + c
                value = dot(local, jnp.concatenate([held[v], up[v]], axis=0))
                if a == 3:
                    value += dot(from_lower, lower[12 * side + c])
                if a == 0:
                    value += dot(from_upper, upper[12 * side + c])
                target[4 * a + c, :, :] = join_fields(value)


def norm_terms(stats, film):
    lines = jnp.sum(stats[...], axis=0)
    total, square = unpack_lines(lines)
    cells = lines[3:4, 0:1]
    mean = total / cells
    variance = square / cells - mean * mean
    inverse = lax.rsqrt(variance + 1e-05)
    scale = 1.0 + film[:, :CHANNELS]
    shift = film[:, CHANNELS:]
    return cells, mean, inverse, scale, shift


def gather_blocks(rule, half, own, low, high, low_y, high_y, padded):
    entries = rule[...]
    col = iota((16, 80), 1)
    hot = []
    for n in range(27):
        column = entries[:, n : n + 1]
        target = jnp.where(column >= 17, column - 1 + half, column)
        target = jnp.where(column >= 25, column + 7 + half, target)
        target = jnp.where(column >= 33, column + 15, target)
        target = jnp.where(column >= 45, column + 19, target)
        hit = (column != 16) & (col == target)
        hot.append(jnp.where(hit, 1.0, 0.0).astype(BF16))
    none = jnp.zeros((16, CHANNELS), BF16)
    for a in range(4):
        for b in range(4):
            for c in range(4):
                mine = own[16 * a + 4 * b + c]
                padded[a + 1, b + 1, c + 1, :, :] = mine
                ways = [
                    [(q + 1, 0)] + ([(5, 1)] if q == 0 else []) + ([(0, -1)] if q == 3 else [])
                    for q in (a, b, c)
                ]
                places = [(x, y, z) for x in ways[0] for y in ways[1] for z in ways[2]][1:]
                if not places:
                    continue
                listed = jnp.concatenate(
                    [
                        mine,
                        low[4 * b + c] if a == 3 else none,
                        high[4 * b + c] if a == 0 else none,
                        low_y[4 * a + c] if b == 3 else none,
                        high_y[4 * a + c] if b == 0 else none,
                    ],
                    axis=0,
                )
                chosen = jnp.concatenate(
                    [hot[9 * (x[1] + 1) + 3 * (y[1] + 1) + z[1] + 1] for x, y, z in places], axis=0
                )
                found = dot(chosen, listed).astype(BF16)
                for m, (x, y, z) in enumerate(places):
                    padded[x[0], y[0], z[0], :, :] = found[16 * m : 16 * m + 16]


def window(padded, k):
    x, y, z = k // 9, (k // 3) % 3, k % 3
    part = padded[pl.ds(x, 4), pl.ds(y, 4), pl.ds(z, 4), :, :]
    return part.reshape(1024, CHANNELS)


def early_kernel(
    up, lower, upper, side_l, side_u, rule, weight_at, film_at, action_at,
    back, turned, film, wide, low_y, high_y, weight, film_weight, action, done,
):
    pairs = ((weight_at, weight), (film_at, film_weight), (action_at, action))
    copies = [
        pltpu.make_async_copy(source, target, done.at[n]) for n, (source, target) in enumerate(pairs)
    ]
    for copy in copies:
        copy.start()
    low_y[...] = one_field(side_l[...], 1)
    high_y[...] = one_field(side_u[...], 1)
    gather_blocks(rule, 8, up, lower, upper, low_y, high_y, wide)
    same = jnp.where(iota((CHANNELS, CHANNELS), 0) == iota((CHANNELS, CHANNELS), 1), 1.0, 0.0)
    turned[...] = dot_nt(same.astype(BF16), up[...].reshape(1024, CHANNELS)).astype(BF16)
    back[...] = jnp.zeros_like(back)
    for copy in copies:
        copy.wait()
    film[...] = lax.dot_general(
        action[...],
        film_weight[...],
        (((1,), (0,)), ((), ())),
        precision=lax.Precision.HIGHEST,
        preferred_element_type=F32,
    )

    def step(t, carry):
        k = 3 * t
        total = dot(window(wide, k), weight[26 - k])
        total += dot(window(wide, k + 1), weight[25 - k])
        back[...] += total + dot(window(wide, k + 2), weight[24 - k])
        return carry

    lax.fori_loop(0, 9, step, 0)


def weight_kernel(
    counts, core, held, lower, upper, side_l, side_u, up_turned, rule, stats, film,
    near, far, padded_at, hid, low, high, low_y, high_y, padded, turned, done,
):
    cells, mean, inverse, scale, shift = norm_terms(stats, film)
    row, col = iota((256, CHANNELS), 0), iota((256, CHANNELS), 1)
    group = ((row >> 4) & 7) * 2 + jnp.where(row >= 128, 1 - core[0], core[0])
    for m in range(4):
        place = (row + 4 * m) & 15
        spread = (place < 12) & (col == group * 12 + place)
        spread = jnp.where(spread, 1.0, 0.0).astype(BF16)
        turned[m, :, :] = dot(spread, up_turned[...]).astype(BF16)

    def act(x):
        x = (x.astype(F32) - mean) * inverse * scale + shift
        return jnp.maximum(x, 0.0)

    live = (iota((256, 1), 0) & 15) < counts[0]
    for g in range(4):
        part = slice(16 * g, 16 * g + 16)
        x = act(held[part, :, :].reshape(256, CHANNELS))
        hid[part, :, :] = jnp.where(live, x, 0.0).astype(BF16).reshape(16, 16, CHANNELS)
    for source, target in (
        (lower[...], low),
        (upper[...], high),
        (one_field(side_l[...], 0), low_y),
        (one_field(side_u[...], 0), high_y),
    ):
        x = act(source.reshape(256, CHANNELS))
        target[...] = x.astype(BF16).reshape(16, 16, CHANNELS)
    gather_blocks(rule, 0, hid, low, high, low_y, high_y, padded)
    out = pltpu.make_async_copy(padded, padded_at, done.at[0])
    out.start()
    line = iota((256, 384), 0) & 15

    def pair(m, k1, k2):
        grad1 = dot(turned[m], window(padded, k1))
        grad2 = dot(turned[m], window(padded, k2)) if k2 is not None else jnp.zeros_like(grad1)
        rest = jnp.concatenate([grad1[:, 128:], grad2[:, 128:]], axis=1)
        return jnp.concatenate([grad1[:, :128], grad2[:, :128], rest], axis=1)

    def store(at, value):
        value = value.astype(BF16).reshape(16, 1, 16, 384)
        near[:, pl.ds(at, 1), :, :] = value[:8]
        far[:, pl.ds(at, 1), :, :] = value[8:]

    def step(q, carry):
        k = 8 * q
        first, second = pair(0, k, k + 1), pair(1, k + 2, k + 3)
        store(3 * q, jnp.where(line < 12, first, second))
        third = pair(2, k + 4, k + 5)
        store(3 * q + 1, jnp.where(line < 8, second, third))
        fourth = pair(3, k + 6, k + 7)
        store(3 * q + 2, jnp.where(line < 4, third, fourth))
        return carry

    lax.fori_loop(0, 3, step, 0)
    first, second = pair(0, 24, 25), pair(1, 26, None)
    store(9, jnp.where(line < 12, first, second))
    store(10, jnp.where(line < 8, second, 0.0))
    out.wait()


def split(value):
    first = value.astype(BF16).astype(F32)
    second = (value - first).astype(BF16).astype(F32)
    return first, second, value - first - second


def slope_kernel(counts, held, up, back, stats, film, kept_at, lines, kept, done):
    cells, mean, inverse, scale, shift = norm_terms(stats, film)
    shift_grad = jnp.zeros((1, CHANNELS), F32)
    scale_grad = jnp.zeros((1, CHANNELS), F32)
    live = (iota((256, 1), 0) & 15) < counts[0]
    for g in range(4):
        at = slice(256 * g, 256 * g + 256)
        part = slice(16 * g, 16 * g + 16)
        x = held[part, :, :].reshape(256, CHANNELS).astype(F32)
        normed = (x - mean) * inverse
        slope = jnp.where(live & (normed * scale + shift > 0), back[at, :], 0.0)
        shift_grad += jnp.sum(slope, axis=0, keepdims=True)
        scale_grad += jnp.sum(slope * normed, axis=0, keepdims=True)
        kept[at, :] = up[part, :, :].reshape(256, CHANNELS).astype(F32) + inverse * (slope * scale)
    out = pltpu.make_async_copy(kept, kept_at, done.at[0])
    out.start()
    row = iota((16, 384), 0)
    block = jnp.zeros((16, 384), F32)
    for e, piece in enumerate(split(jnp.concatenate([scale_grad, shift_grad], axis=1))):
        block = jnp.where(row == 8 + e, piece, block)
    lines[...] = block
    out.wait()


def forward_kernel(
    counts, held, weight_at, padded_at, output, token, acc, weight, padded, done,
):
    token[...] = jnp.zeros_like(token)
    copies = [
        pltpu.make_async_copy(weight_at, weight, done.at[0]),
        pltpu.make_async_copy(padded_at, padded, done.at[1]),
    ]
    for copy in copies:
        copy.start()
    acc[...] = jnp.zeros_like(acc)
    for copy in copies:
        copy.wait()

    def step(t, carry):
        k = 3 * t
        total = dot_nt(window(padded, k), weight[k])
        total += dot_nt(window(padded, k + 1), weight[k + 1])
        acc[...] += total + dot_nt(window(padded, k + 2), weight[k + 2])
        return carry

    lax.fori_loop(0, 9, step, 0)
    swap = swap_matrix(None)
    live = (iota((256, 1), 0) & 15) < counts[0]
    for g in range(4):
        part = slice(16 * g, 16 * g + 16)
        x = held[part, :, :].reshape(256, CHANNELS).astype(F32)
        mixed = jnp.where(live, x + acc[256 * g : 256 * g + 256, :], 0.0).astype(BF16)
        output[:, part, :] = dot(swap, mixed).astype(BF16).reshape(16, 16, CHANNELS)


def place_of(share):
    return (share // 3, share % 3) if share < 30 else (10, 2 * (share - 30))


def share_kernel(parts, token, shares):
    for tile in reversed(range(TILES)):
        total = jnp.sum(parts[:, tile, :, :].astype(F32), axis=0)
        if tile == TILES - 1:
            sums = total[8:9] + total[9:10] + total[10:11]
            pieces = split(sums)[:2]
            lines = [piece[:, 128 * m : 128 * m + 128] for piece in pieces for m in range(3)]
            block = stack_lines(lines, 8)
        for share in range(32):
            if place_of(share)[0] == tile:
                third = place_of(share)[1]
                mine = total[:, 128 * third : 128 * third + 128]
                shares[share, :, :] = jnp.concatenate([mine, block], axis=0).astype(BF16)


def own_kernel(parts, mine, sums):
    total = jnp.sum(parts[...].astype(F32), axis=0)
    for i in range(mine.shape[0]):
        mine[i, :, :] = total[0:16].astype(BF16)
    lines = total[16:19] + total[19:22]
    sums[...] = jnp.concatenate([lines[0:1], lines[1:2], lines[2:3]], axis=1)


def finish_kernel(
    counts, sums, other, stats, film, action, held, kept_at, grad_film, grad_inputs, kept, done,
):
    copy = pltpu.make_async_copy(kept_at, kept, done.at[0])
    copy.start()
    total = sums[...] + other[...]
    scale_grad, shift_grad = total[:, :CHANNELS], total[:, CHANNELS:]
    cells, mean, inverse, scale, shift = norm_terms(stats, film)
    grad_film[:, :CHANNELS] = action[...] * scale_grad
    grad_film[:, CHANNELS:] = action[...] * shift_grad
    swap = swap_matrix(None)
    live = (iota((256, 1), 0) & 15) < counts[0]
    copy.wait()
    for g in range(4):
        part = slice(16 * g, 16 * g + 16)
        x = held[part, :, :].reshape(256, CHANNELS).astype(F32)
        normed = (x - mean) * inverse
        value = kept[256 * g : 256 * g + 256, :] - inverse * (
            scale * shift_grad / cells + normed * scale * scale_grad / cells
        )
        value = jnp.where(live, value, 0.0).astype(BF16)
        grad_inputs[:, part, :] = dot(swap, value).astype(BF16).reshape(16, 16, CHANNELS)


def unpack_kernel(tiles, grad_weight):
    zero = jnp.zeros((16, 128), BF16)
    thirds = [
        jnp.concatenate([tiles[3 * u + n] for u in range(10)] + [last], axis=0)
        for n, last in enumerate((tiles[30], zero, tiles[31]))
    ]
    even = jnp.concatenate([thirds[0], thirds[2][:, :64]], axis=1)
    odd = jnp.concatenate([thirds[1], thirds[2][:, 64:]], axis=1)
    row, col = iota((384, 352), 0), iota((384, 352), 1)
    k = row & 31
    chosen = (k < 27) & (col == (row >> 5) + 12 * (k >> 1) + 176 * (k & 1))
    chosen = jnp.where(chosen, 1.0, 0.0).astype(BF16)
    found = dot(chosen, jnp.concatenate([even, odd], axis=0)).reshape(12, 32, CHANNELS)
    grad_weight[...] = found[:, :27, :]


SMEM = pl.BlockSpec(memory_space=pltpu.SMEM)
VMEM = pl.BlockSpec(memory_space=pltpu.VMEM)
ANY = pl.BlockSpec(memory_space=pl.ANY)


def call(kernel, scalars, arrays, outs, scratch=(), flops=0, name=None, left=0, room=12, copies=0):
    split_at = len(arrays) - left
    arrays = list(arrays[:split_at]) + [
        pltpu.with_memory_space_constraint(x, pltpu.HBM) for x in arrays[split_at:]
    ]
    moved = sum(x.size * x.dtype.itemsize for x in arrays)
    shapes, specs = [], []
    for shape, dtype, *marked in outs:
        moved += math.prod(shape) * jnp.dtype(dtype).itemsize
        shapes.append(pltpu.HBM(shape, dtype) if marked else jax.ShapeDtypeStruct(shape, dtype))
        specs.append(ANY if marked else VMEM)
    return pl.pallas_call(
        kernel,
        out_shape=shapes,
        in_specs=[SMEM] * len(scalars) + [VMEM] * split_at + [ANY] * left,
        out_specs=specs,
        scratch_shapes=[pltpu.VMEM(*s) for s in scratch]
        + ([pltpu.SemaphoreType.DMA((copies,))] if copies else []),
        compiler_params=pltpu.CompilerParams(vmem_limit_bytes=room * MIB),
        cost_estimate=pl.CostEstimate(flops=flops, bytes_accessed=moved, transcendentals=0),
        name=name,
    )(*scalars, *arrays)


def exchange(array, axis, groups=None):
    return lax.all_to_all(array, axis, 0, 0, axis_index_groups=groups, tiled=True)


def body(features, cotangent, counts, neighbours, send_x, send_y, action, conv_weight, film_weight):
    size_x, size_y = lax.axis_size("gx"), lax.axis_size("gy")
    count = counts.reshape(1)
    rule = neighbours[0, 0]
    list_x = pltpu.with_memory_space_constraint(send_x[0, 0], pltpu.HBM)
    block = ((VOXELS, 16, CHANNELS), BF16)
    face = ((16, 16, CHANNELS), BF16)
    spaced = ((6, 6, 6, 16, CHANNELS), BF16)
    joined = ((16, 16, 384), BF16)
    held, up, stats, face_low, face_high = call(
        pack_kernel,
        [count, list_x],
        [features[0, 0], cotangent[0, 0]],
        [block, block, ((size_x, 4, 128), F32), face, face],
        [((SLOTS, VOXELS, CHANNELS), BF16), ((SLOTS, VOXELS, CHANNELS), BF16)],
        flops=10**9,
        name="pack",
        left=2,
        copies=2,
    )
    up_x = [(i, i + 1) for i in range(size_x - 1)]
    down_x = [(i + 1, i) for i in range(size_x - 1)]
    up_y = [(i, i + 1) for i in range(size_y - 1)]
    down_y = [(i + 1, i) for i in range(size_y - 1)]
    lower = lax.ppermute(face_high, "gx", up_x)
    upper = lax.ppermute(face_low, "gx", down_x)
    stats = exchange(stats, "gx")
    weight = jnp.transpose(conv_weight, (1, 0, 2))
    face_low, face_high, stats = call(
        cross_kernel,
        [send_y[0, 0]],
        [held, up, lower, upper, stats],
        [joined, joined, ((size_y, 4, 128), F32)],
        flops=10**8,
        name="cross",
    )
    side_l = lax.ppermute(face_high, "gy", up_y)
    side_u = lax.ppermute(face_low, "gy", down_y)
    stats = exchange(stats, "gy")
    core = lax.axis_index("gx") & 1
    swapped = [(i, i ^ 1) for i in range(size_x)]
    taps = ((27, CHANNELS, CHANNELS), BF16)
    total = ((1024, CHANNELS), F32)
    back, turned, film = call(
        early_kernel,
        [],
        [up, lower, upper, side_l, side_u, rule, weight, film_weight, action[None]],
        [total, ((CHANNELS, 1024), BF16), ((1, 2 * CHANNELS), F32)],
        [spaced, face, face, taps, ((128, 2 * CHANNELS), F32), ((1, 128), F32)],
        flops=3 * 10**9,
        name="early",
        left=3,
        copies=3,
        room=20,
    )
    half = ((8, TILES, 16, 384), BF16)
    near, far, padded = call(
        weight_kernel,
        [count, core.reshape(1)],
        [held, lower, upper, side_l, side_u, turned, rule, stats, film],
        [half, half, (*spaced, True)],
        [block, face, face, face, face, spaced, ((4, 256, 1024), BF16)],
        flops=4 * 10**9,
        name="weight",
        copies=1,
        room=20,
    )
    other = lax.ppermute(far, "gx", swapped)
    kept, lines = call(
        slope_kernel,
        [count],
        [held, up, back, stats, film],
        [(*total, True), ((16, 384), F32)],
        [total],
        flops=10**8,
        name="slope",
        copies=1,
    )
    tile = lax.broadcasted_iota(jnp.int32, half[0], 1)
    row = lax.broadcasted_iota(jnp.int32, half[0], 2)
    parts = near.astype(F32) + other.astype(F32)
    parts = jnp.where((tile == TILES - 1) & (row >= 8), lines, parts).astype(BF16)
    parts = exchange(parts, "gx", [list(range(c, size_x, 2)) for c in range(2)])
    output, token = call(
        forward_kernel,
        [count],
        [held, weight, padded],
        [((SLOTS, VOXELS, CHANNELS), BF16), ((8, 128), F32)],
        [total, taps, spaced],
        flops=3 * 10**9,
        name="forward",
        left=2,
        copies=2,
        room=16,
    )
    (shares,) = call(share_kernel, [], [parts, token], [((size_y, 24, 128), BF16)], name="share")
    shares = exchange(shares, "gy")
    mine, sums = call(
        own_kernel, [], [shares], [((size_y, 16, 128), BF16), ((1, 2 * CHANNELS), F32)], name="own"
    )
    other = lax.ppermute(sums, "gx", swapped)
    tiles = exchange(mine, "gy")
    grad_film, grad_inputs = call(
        finish_kernel,
        [count],
        [sums, other, stats, film, action[:, None], held, kept],
        [((128, 2 * CHANNELS), F32), ((SLOTS, VOXELS, CHANNELS), BF16)],
        [total],
        flops=10**9,
        name="finish",
        left=1,
        copies=1,
    )
    (grad_weight,) = call(unpack_kernel, [], [tiles], [((12, 27, CHANNELS), F32)], name="unpack")
    return output[None, None], grad_inputs[None, None], grad_weight, grad_film


def solution(mesh):
    tile = P("gx", "gy")
    return jax.shard_map(
        body,
        mesh=mesh,
        in_specs=(tile, tile, tile, tile, tile, tile, P(), P(), P()),
        out_specs=(tile, tile, P("gx"), P()),
        check_vma=False,
    )
```
